512 devices in a mesh: rep: 8 (over y), ep: 64 (over x, z, core).
Axes of the slice: x: 4, y: 8, z: 8, core: 2. Of those that a mesh axis runs over, the one named last changes fastest.
Arguments:
- master: float32 [3, 2048, 16384], P(None, ('rep', 'ep')), may hold values from -0.125 to 0.125
- moment_one: float32 [3, 2048, 16384], P(None, ('rep', 'ep')), may hold values from -0.02 to 0.02
- moment_two: float32 [3, 2048, 16384], P(None, ('rep', 'ep')), may hold values from 1e-05 to 0.0001
- gradient: bfloat16 [3, 2048, 16384], P(None, ('rep', 'ep')), may hold values from -0.079589844 to 0.079589844
- states: bfloat16 [2048, 2048], P(('rep', 'ep')), may hold values from -6 to 6
- norm_gain: float32 [2048], replicated, may hold values from 0.5 to 1.5
- routes: int32 [2048, 8], P(('rep', 'ep')), may hold values from 0 to 15, all different within a row; in each aligned block of 4 rows (0 to 3, 4 to 7, ...) at most 3 rows name the same one
- route_weights: float32 [2048, 8], P(('rep', 'ep')), may hold values from 0.05 to 1
Outputs:
- master_next: float32 [3, 2048, 16384], P(None, ('rep', 'ep'))
- mixture: bfloat16 [2048, 2048], P(('rep', 'ep'))
The draws below stay inside these ranges and needn't reach their ends.
Inputs may be any that keep to these rules, and one draw needn't show every extreme that they name: `routes`: each row names 8 distinct experts. Within the 4 rows of one device no expert is named more than 3 times, and in some device's rows some expert is named exactly 3 times.
All inputs are finite; a program needn't handle non-finite values.
Results may differ from the reference program's by a relative error of at most 0.01005.
Values may be sent and summed in bfloat16 or wider, within the bound.
No kernel may reach another device: no remote copies, remote signals or barrier semaphores. Data moves between devices by JAX's collectives and lax.ppermute only.
A program may use at most 128 MiB of HBM per device.

```python
import math
import jax
import jax.numpy as jnp
import numpy as np
from jax import lax

D = 2048
F = 1024
E = 16
TOP = 8
QBLOCK = 128
STEP = 10
TOK_DEV = 4
CAP = 3
ROWS = 2048
EF = 16384
N_REP = 8
N_EP = 64


def levels(key, shape, cuts, low, high):
    def one(dim, blocks):
        steps = jax.random.uniform(jax.random.fold_in(jax.random.fold_in(key, 6), dim), (blocks,), jnp.float32, low / len(cuts), high / len(cuts))
        return jnp.repeat(jnp.exp(steps), shape[dim] // blocks).reshape((-1,) + (1,) * (len(shape) - dim - 1))

    level = one(*cuts[0])
    for cut in cuts[1:]:
        level = level * one(*cut)
    return level


def assign_block(stream_key, own, number, rows, count, top, most, slope):
    ranking = jax.random.permutation(stream_key, count)
    packed, common = portions_of(count, rows * top, most, slope, True), portions_of(count, rows * top, most, slope, False)
    places = jnp.arange(count)

    def named(sizes, turn):
        used = int((sizes > 0).sum())
        fixed = max(1, used // 4)
        moved = fixed + (places - fixed + turn * (used - fixed)) % max(1, count - fixed)
        return jnp.zeros((count,), jnp.int32).at[ranking[jnp.where(places < fixed, places, moved)]].set(jnp.asarray(sizes, jnp.int32))

    sizes = jnp.where(number % 4 == 0, named(packed, number // 4), named(common, number - number // 4 - 1))
    mixed = jax.random.permutation(jax.random.fold_in(own, 3), count)
    source_of, sink = mixed[0:count // 2 * 2:2], mixed[1:count // 2 * 2:2]
    slack = jnp.minimum(sizes[source_of] - 1, most - sizes[sink]) // 2
    slack = jnp.where((source_of == ranking[0]) | (sink == ranking[0]) | (sizes[sink] == 0), 0, jnp.maximum(slack, 0))
    moved = jax.random.randint(jax.random.fold_in(own, 4), (count // 2,), 0, 1 << 20) % (slack + 1)
    sizes = sizes.at[source_of].add(-moved).at[sink].add(moved)
    labels = jnp.searchsorted(jnp.cumsum(sizes), jnp.arange(rows * top), side="right").astype(jnp.int32)
    listing = labels.reshape(top, rows).T
    listing = listing[jax.random.permutation(jax.random.fold_in(own, 1), rows)]
    turn = jax.random.randint(jax.random.fold_in(own, 2), (rows, 1), 0, top)
    return jnp.take_along_axis(listing, (jnp.arange(top)[None, :] + turn) % top, axis=1)


def portions_of(number_of, total, most, lean, full):
    weights = [(1 << 20) // math.isqrt(grade ** lean) + 1 for grade in range(1, number_of + 1)]
    largest = most if full else min(most, max(-(-total // number_of), total * weights[0] // sum(weights)))
    least = 1 if total - largest >= number_of - 1 else 0
    holding, surplus = [largest] + [least] * (number_of - 1), total - largest - least * (number_of - 1)
    while surplus > 0:
        free = [i for i in range(1, number_of) if holding[i] < largest] or [i for i in range(1, number_of) if holding[i] < most]
        whole, left = sum([weights[i] for i in free]), surplus
        for i in free:
            extra = min(most - holding[i], max(1, left * weights[i] // whole), surplus)
            holding[i] = holding[i] + extra
            surplus = surplus - extra
    return np.array(holding)


def bell_draw(rng, shape, deviation, reach, pieces=(), kind=jnp.bfloat16):
    gain = levels(rng, shape, pieces, -0.22, 0.18) if pieces else 1.0
    array = jax.random.normal(rng, shape, jnp.float32) * deviation * gain
    return jnp.minimum(jnp.maximum(array, -reach), reach).astype(kind)


def setup_inputs(seed: int = 0) -> dict:
    arg_keys = jax.random.split(jax.random.key(seed), 9)
    master = bell_draw(arg_keys[0], (3, D, EF), D ** -0.5, 0.125, ((1, 512),), jnp.float32)
    moment_one = bell_draw(arg_keys[1], (3, D, EF), 0.003, 0.02, ((1, 512),), jnp.float32)
    moment_two = jnp.clip(jnp.exp(math.log(0.0001) - 2.3025851 * jax.random.uniform(arg_keys[2], (3, D, EF), jnp.float32) ** levels(arg_keys[2], (3, D, EF), ((1, 512),), -0.2, 0.2)), 9.999999747378752e-06, 0.0001)
    gradient = bell_draw(arg_keys[3], (3, D, EF), 0.01, 0.079589844, ((1, 512),))
    states = bell_draw(arg_keys[4], (ROWS, D), 1.0, 6.0, ((0, 512),))
    norm_gain = jnp.clip(1.0 + 0.1 * jax.random.normal(arg_keys[5], (D,), jnp.float32), 0.5, 1.5)
    routes_keys = jax.random.split(jax.random.fold_in(arg_keys[6], 1), ROWS // TOK_DEV)
    routes_turns = jax.random.permutation(jax.random.fold_in(arg_keys[6], 3), ROWS // TOK_DEV)
    routes = jax.vmap(lambda own, number: assign_block(jax.random.fold_in(arg_keys[6], 2), own, number, TOK_DEV, E, TOP, CAP, 2))(routes_keys, routes_turns).reshape((ROWS, TOP))
    route_weights = jnp.clip(0.05 + 0.95 * jax.random.uniform(arg_keys[7], (ROWS, TOP), jnp.float32) ** levels(arg_keys[7], (ROWS, TOP), ((0, 512),), -0.2, 0.2), 0.05, 1.0)
    return dict(master=master, moment_one=moment_one, moment_two=moment_two, gradient=gradient, states=states, norm_gain=norm_gain, routes=routes, route_weights=route_weights)


BETA_ONE = 0.9
BETA_TWO = 0.95
LEARN_RATE = 0.01
ADAM_EPSILON = 1e-08
WEIGHT_DECAY = 0.1
SATURATION = 448.0
SCALE_EPSILON = 1e-06
NORM_EPSILON = 1e-06
SUBNORMAL_EDGE = 0.015625
MANTISSA_BITS = 3.0

def adam_update(master, moment_one, moment_two, gradient):
    grad_float = gradient.astype(jnp.float32)
    first = BETA_ONE * moment_one + (1.0 - BETA_ONE) * grad_float
    second = BETA_TWO * moment_two + (1.0 - BETA_TWO) * grad_float * grad_float
    correct_one = 1.0 - BETA_ONE ** STEP
    correct_two = 1.0 - BETA_TWO ** STEP
    direction = first / correct_one / (jnp.sqrt(second / correct_two) + ADAM_EPSILON)
    return master - LEARN_RATE * (direction + WEIGHT_DECAY * master)

def block_max(weights, block_size):
    stacked = weights.shape[0]
    columns = weights.shape[2]
    magnitude = jnp.abs(weights).reshape(stacked, weights.shape[1], columns // block_size, block_size)
    return lax.optimization_barrier(jnp.max(magnitude, axis=(1, 3)))

def column_scale(largest, block_size):
    return jnp.repeat((largest + SCALE_EPSILON) / SATURATION, block_size, axis=1)

def minifloat_grid(values):
    magnitude = jnp.abs(values)
    exponent = jnp.floor(jnp.log2(jnp.maximum(magnitude, SUBNORMAL_EDGE)))
    spacing = jnp.exp2(exponent - MANTISSA_BITS)
    snapped = jnp.floor(magnitude / spacing + 0.5) * spacing
    return jnp.sign(values) * snapped

def quantize(weights, scales):
    clipped = jnp.clip(weights / scales[:, None, :], -SATURATION, SATURATION)
    return minifloat_grid(clipped).astype(jnp.bfloat16)

def rms_norm(states, norm_gain):
    values = states.astype(jnp.float32)
    mean_square = lax.optimization_barrier(jnp.mean(values * values, axis=1, keepdims=True))
    return (values * lax.rsqrt(mean_square + NORM_EPSILON) * norm_gain[None, :]).astype(jnp.bfloat16)

def reference(master, moment_one, moment_two, gradient, states, norm_gain, routes, route_weights):
    updated = adam_update(master, moment_one, moment_two, gradient)
    scales = column_scale(block_max(updated, QBLOCK), QBLOCK)
    payload = quantize(updated, scales)
    normed = rms_norm(states, norm_gain)
    weights = route_weights / lax.optimization_barrier(jnp.sum(route_weights, axis=1, keepdims=True))
    devices = N_REP * N_EP
    hidden_width = E * F // N_EP
    blocks = F // hidden_width
    per_device = routes.reshape(devices, TOK_DEV * TOP)
    onehot = (per_device[:, :, None] == jnp.arange(E, dtype=jnp.int32)[None, None, :]).astype(jnp.int32)
    earlier = jnp.cumsum(onehot, axis=1) - onehot
    slot_index = lax.optimization_barrier(jnp.sum(earlier * onehot, axis=2))
    device_ids = (jnp.arange(devices, dtype=jnp.int32) * CAP)[:, None]
    position = (device_ids + slot_index).reshape(-1)
    row_ids = jnp.repeat(jnp.arange(ROWS, dtype=jnp.int32), TOP)
    expert_flat = routes.reshape(-1)
    table = jnp.full((E, devices * CAP), ROWS, jnp.int32).at[expert_flat, position].set(row_ids)
    weight_table = jnp.zeros((E, devices * CAP), jnp.float32).at[expert_flat, position].set(weights.reshape(-1))
    padded = jnp.concatenate([normed, jnp.zeros((1, D), jnp.bfloat16)], axis=0)

    def expert_pass(totals, expert):
        table_row = table[expert]
        token_rows = padded[table_row]
        columns = lax.dynamic_slice_in_dim(payload, expert * F, F, 2)
        colscales = lax.dynamic_slice_in_dim(scales, expert * F, F, 1)
        gate_act = jnp.dot(token_rows, columns[0], preferred_element_type=jnp.float32) * colscales[0][None, :]
        up_act = jnp.dot(token_rows, columns[1], preferred_element_type=jnp.float32) * colscales[1][None, :]
        hidden = (jax.nn.silu(gate_act) * up_act * colscales[2][None, :]).astype(jnp.bfloat16)
        count = token_rows.shape[0]
        hidden_blocks = hidden.reshape(count, blocks, hidden_width).astype(jnp.float32)
        down_blocks = columns[2].reshape(D, blocks, hidden_width).astype(jnp.float32)
        partial_value = jnp.einsum('nbh,dbh->nbd', hidden_blocks, down_blocks).astype(jnp.bfloat16)
        expert_out = lax.optimization_barrier(jnp.sum(partial_value.astype(jnp.float32), axis=1))
        totals = totals.at[table_row].add(weight_table[expert][:, None] * expert_out, mode='drop')
        return (totals, None)
    totals, unused = lax.scan(expert_pass, jnp.zeros((ROWS, D), jnp.float32), jnp.arange(E, dtype=jnp.int32))
    return (updated, totals.astype(jnp.bfloat16))
```

```python
import jax
import jax.numpy as jnp
from jax import lax
from jax.experimental import pallas as pl
from jax.experimental.pallas import tpu as pltpu
from jax.sharding import Mesh, PartitionSpec as P

E = 16
TOP = 8
QBLOCK = 128
STEP = 10
CAP = 3

BETA_ONE = 0.9
BETA_TWO = 0.95
LEARN_RATE = 0.01
ADAM_EPSILON = 1e-08
WEIGHT_DECAY = 0.1
SATURATION = 448.0
SCALE_EPSILON = 1e-06
NORM_EPSILON = 1e-06
SUBNORMAL_EDGE = 0.015625

BOUND = 0.1875
LEVELS = 32767.0
UNIT = BOUND / LEVELS**5

AXES = ("y", "x", "z", "c")
OWNERS = ("y", "z")
COPIES = ("x", "c")


def adam_update(master, moment_one, moment_two, gradient):
    grad_float = gradient.astype(jnp.float32)
    first = BETA_ONE * moment_one + (1.0 - BETA_ONE) * grad_float
    second = BETA_TWO * moment_two + (1.0 - BETA_TWO) * grad_float * grad_float
    correct_one = 1.0 - BETA_ONE**STEP
    correct_two = 1.0 - BETA_TWO**STEP
    direction = first / correct_one / (jnp.sqrt(second / correct_two) + ADAM_EPSILON)
    return master - LEARN_RATE * (direction + WEIGHT_DECAY * master)


def encode(weights):
    magnitude = jnp.abs(weights) * (1.0 / BOUND)
    level = jnp.floor(jnp.exp2(jnp.log2(magnitude) * 0.2) * LEVELS + 0.5)
    level = jnp.where(magnitude > 0, jnp.minimum(level, LEVELS), 0.0)
    return jnp.where(weights < 0, -level, level).astype(jnp.int32).astype(jnp.int16)


def rms_norm(states, norm_gain):
    values = states.astype(jnp.float32)
    mean_square = jnp.mean(values * values, axis=1, keepdims=True)
    return (values * lax.rsqrt(mean_square + NORM_EPSILON) * norm_gain[None, :]).astype(
        jnp.bfloat16
    )


def snap(q):
    scaled = q * 1048577.0
    normal = scaled - (scaled - q)
    small = (q + 24576.0) - 24576.0
    return jnp.where(jnp.abs(q) < SUBNORMAL_EDGE, small, normal)


def expert_kernel(codes, tokens, out, packed):
    copies, sources = codes.shape[0], codes.shape[1]
    xs = copies // 2
    groups = sources // 8

    def extremes(step, carry):
        high, low = carry
        p = step // groups
        y = step % groups
        block = codes[p, pl.ds(y * 8, 8)].astype(jnp.int32)
        return jnp.maximum(high, jnp.max(block, axis=0)), jnp.minimum(low, jnp.min(block, axis=0))

    zero = jnp.zeros((3, 8, 128), jnp.int32)
    high, low = lax.fori_loop(0, copies * groups, extremes, (zero, zero))
    top = jnp.maximum(high, -low).astype(jnp.float32)
    sub = lax.broadcasted_iota(jnp.int32, (8, 128), 0)
    scales = []
    factors = []
    for m in range(3):
        pair = []
        for h in range(2):
            level = jnp.max(
                jnp.max(top[m, 4 * h : 4 * h + 4], axis=0, keepdims=True), axis=1, keepdims=True
            )
            square = level * level
            largest = square * square * level * UNIT
            pair.append((largest + SCALE_EPSILON) / SATURATION)
        scales.append(
            jnp.concatenate([jnp.broadcast_to(v, (1, 128)) for v in pair], axis=1)
        )
        factors.append(
            jnp.where(
                sub < 4,
                jnp.broadcast_to(UNIT / pair[0], (8, 128)),
                jnp.broadcast_to(UNIT / pair[1], (8, 128)),
            )
        )

    def quantize(m):
        factor = factors[m][None]

        def values(p, y):
            level = codes[p, pl.ds(y * 8, 8), m].astype(jnp.int32).astype(jnp.float32)
            square = level * level
            q = square * square * level * factor
            return snap(jnp.clip(q, -SATURATION, SATURATION))

        def step(t, carry):
            y = t // xs
            x = t % xs
            even = values(2 * x, y)
            odd = values(2 * x + 1, y)
            first_half = (lax.broadcasted_iota(jnp.int32, even.shape, 1)) < 4
            left = jnp.where(first_half, even, pltpu.roll(odd, 4, 1))
            right = jnp.where(first_half, pltpu.roll(even, 4, 1), odd)
            rows = pl.ds(pl.multiple_of(t * 64, 64), 64)
            packed[m, rows, 0:128] = left.reshape(64, 128).astype(jnp.bfloat16)
            packed[m, rows, 128:256] = right.reshape(64, 128).astype(jnp.bfloat16)
            return carry

        lax.fori_loop(0, xs * groups, step, 0)

    for m in range(3):
        quantize(m)
    token_rows = tokens[...]
    gate_act = jnp.dot(token_rows, packed[0], preferred_element_type=jnp.float32) * scales[0]
    up_act = jnp.dot(token_rows, packed[1], preferred_element_type=jnp.float32) * scales[1]
    hidden = gate_act / (1.0 + jnp.exp(-gate_act)) * up_act * scales[2]
    out[...] = lax.dot_general(
        hidden.astype(jnp.bfloat16),
        packed[2],
        (((1,), (1,)), ((), ())),
        preferred_element_type=jnp.float32,
    ).astype(jnp.bfloat16)


def experts(codes, tokens):
    width = tokens.shape[1]
    return pl.pallas_call(
        expert_kernel,
        out_shape=jax.ShapeDtypeStruct(tokens.shape, jnp.bfloat16),
        in_specs=[pl.BlockSpec(memory_space=pltpu.VMEM)] * 2,
        out_specs=pl.BlockSpec(memory_space=pltpu.VMEM),
        scratch_shapes=[pltpu.VMEM((3, width, 256), jnp.bfloat16)],
        compiler_params=pltpu.CompilerParams(vmem_limit_bytes=40 * 2**20),
    )(codes, tokens)


def body(master, moment_one, moment_two, gradient, states, norm_gain, routes, route_weights):
    owners = lax.axis_size(OWNERS)
    updated = adam_update(master, moment_one, moment_two, gradient)
    codes = encode(updated)
    codes = codes.reshape(3, 4, owners, 2, 128).transpose(2, 0, 3, 1, 4).reshape(owners, 3, 8, 128)
    columns = lax.all_to_all(codes, OWNERS, split_axis=0, concat_axis=0, tiled=True)
    gathered_codes = lax.all_gather(columns, COPIES, axis=0, tiled=False)

    normed = rms_norm(states, norm_gain)
    weights = route_weights / jnp.sum(route_weights, axis=1, keepdims=True)
    row_count = routes.shape[0]
    group_size = owners // E
    expert_ids = routes.reshape(-1)
    onehot = (expert_ids[:, None] == jnp.arange(E, dtype=jnp.int32)[None, :]).astype(jnp.int32)
    earlier = jnp.cumsum(onehot, axis=0) - onehot
    slot_index = jnp.sum(earlier * onehot, axis=1)
    position = expert_ids * CAP + slot_index
    placed = (position[:, None] == jnp.arange(E * CAP, dtype=jnp.int32)[None, :]).astype(
        jnp.float32
    )
    placed = placed.reshape(row_count, TOP, E * CAP)
    select = jnp.sum(placed, axis=1).astype(jnp.bfloat16)
    weighted = jnp.sum(placed * weights[:, :, None], axis=1)
    gathered = lax.dot_general(
        select, normed, (((0,), (0,)), ((), ())), preferred_element_type=jnp.float32
    )
    width = normed.shape[1]
    gathered = gathered.astype(jnp.bfloat16).reshape(E, CAP, width)
    buffer = jnp.repeat(gathered, group_size, axis=0)
    received = lax.all_to_all(buffer, OWNERS, split_axis=0, concat_axis=0, tiled=True)
    tokens = received.reshape(owners * CAP, width)

    partial_value = experts(gathered_codes, tokens).reshape(owners, CAP, width)
    returned = lax.all_to_all(partial_value, OWNERS, split_axis=0, concat_axis=0, tiled=True)
    expert_out = jnp.sum(
        returned.astype(jnp.float32).reshape(E, group_size, CAP, width), axis=1
    )
    expert_out = expert_out.reshape(E * CAP, width)
    mixture = jnp.dot(
        weighted, expert_out, precision=lax.Precision.HIGHEST, preferred_element_type=jnp.float32
    )
    return (updated, mixture.astype(jnp.bfloat16))


def solution(mesh):
    chips = Mesh(mesh.devices.reshape(8, 4, 8, 2), AXES)
    rows = P(None, AXES, None)
    return jax.shard_map(
        body,
        mesh=chips,
        in_specs=(rows, rows, rows, rows, P(AXES, None), P(), P(AXES, None), P(AXES, None)),
        out_specs=(rows, P(AXES, None)),
        check_vma=False,
    )
```

```python
import jax
import jax.numpy as jnp
from jax import lax
from jax.experimental import pallas as pl
from jax.experimental.pallas import tpu as pltpu
from jax.sharding import Mesh, PartitionSpec as P

E = 16
TOP = 8
QBLOCK = 128
STEP = 10
CAP = 3

BETA_ONE = 0.9
BETA_TWO = 0.95
LEARN_RATE = 0.01
ADAM_EPSILON = 1e-08
WEIGHT_DECAY = 0.1
SATURATION = 448.0
SCALE_EPSILON = 1e-06
NORM_EPSILON = 1e-06
SUBNORMAL_EDGE = 0.015625

BOUND = 0.1875
LEVELS = 32767.0
UNIT = BOUND / LEVELS**5

AXES = ("yh", "yl", "x", "zh", "zl", "c")
OWNERS = ("yh", "zh", "yl", "zl")
EXPERTS = ("yh", "zh")
QUARTERS = ("yl", "zl")
HOMES = ("yl", "zl", "yh", "zh")
COPIES = ("x", "c")


def adam_tile(master, moment_one, moment_two, grad_float):
    first = BETA_ONE * moment_one + (1.0 - BETA_ONE) * grad_float
    second = BETA_TWO * moment_two + (1.0 - BETA_TWO) * grad_float * grad_float
    correct_one = 1.0 - BETA_ONE**STEP
    correct_two = 1.0 - BETA_TWO**STEP
    direction = first * (1.0 / correct_one) / (
        jnp.sqrt(second * (1.0 / correct_two)) + ADAM_EPSILON
    )
    return master - LEARN_RATE * (direction + WEIGHT_DECAY * master)


def encode(weights):
    magnitude = jnp.maximum(jnp.abs(weights) * (1.0 / BOUND), 1e-30)
    level = jnp.minimum(jnp.exp2(jnp.log2(magnitude) * 0.2) * LEVELS + 0.5, LEVELS)
    return jnp.where(weights < 0, -level, level).astype(jnp.int32).astype(jnp.int16)


def adam_kernel(master, moment_one, moment_two, gradient, updated, codes):
    for d in range(codes.shape[0]):
        left = slice(d * 256, d * 256 + 128)
        right = slice(d * 256 + 128, d * 256 + 256)
        for m in range(3):

            def tile(ref):
                return jnp.concatenate(
                    [ref[m, :, left].astype(jnp.float32), ref[m, :, right].astype(jnp.float32)],
                    axis=0,
                )

            value = adam_tile(tile(master), tile(moment_one), tile(moment_two), tile(gradient))
            updated[m, :, left] = value[0:4]
            updated[m, :, right] = value[4:8]
            codes[d, m] = encode(value)


def adam_update(master, moment_one, moment_two, gradient, owners):
    steps = 8
    columns = master.shape[2] // steps
    rows = pl.BlockSpec((3, 4, columns), lambda i: (0, 0, i))
    return pl.pallas_call(
        adam_kernel,
        grid=(steps,),
        out_shape=(
            jax.ShapeDtypeStruct(master.shape, jnp.float32),
            jax.ShapeDtypeStruct((owners, 3, 8, 128), jnp.int16),
        ),
        in_specs=[rows] * 4,
        out_specs=(rows, pl.BlockSpec((owners // steps, 3, 8, 128), lambda i: (i, 0, 0, 0))),
    )(master, moment_one, moment_two, gradient)


def rms_norm(states, norm_gain):
    values = states.astype(jnp.float32)
    mean_square = jnp.mean(values * values, axis=1, keepdims=True)
    return (values * lax.rsqrt(mean_square + NORM_EPSILON) * norm_gain[None, :]).astype(
        jnp.bfloat16
    )


def snap(q):
    scaled = q * 1048577.0
    normal = scaled - (scaled - q)
    small = (q + 24576.0) - 24576.0
    return jnp.where(jnp.abs(q) < SUBNORMAL_EDGE, small, normal)


def expert_kernel(quarter, codes, tokens, out, packed, spread):
    copies = codes.shape[0]
    xs, yhs, zhs = copies // 2, codes.shape[1], codes.shape[2]

    def extremes(step, carry):
        high, low = carry
        p = step // yhs
        yh = step % yhs
        block = codes[p, yh].astype(jnp.int32).reshape(zhs * 4, 3, 8, 128)
        return jnp.maximum(high, jnp.max(block, axis=0)), jnp.minimum(low, jnp.min(block, axis=0))

    zero = jnp.zeros((3, 8, 128), jnp.int32)
    high, low = lax.fori_loop(0, copies * yhs, extremes, (zero, zero))
    top = jnp.maximum(high, -low).astype(jnp.float32)
    sub = lax.broadcasted_iota(jnp.int32, (8, 128), 0)
    scales = []
    factors = []
    for m in range(3):
        pair = []
        for h in range(2):
            level = jnp.max(
                jnp.max(top[m, 4 * h : 4 * h + 4], axis=0, keepdims=True), axis=1, keepdims=True
            )
            square = level * level
            largest = square * square * level * UNIT
            pair.append((largest + SCALE_EPSILON) / SATURATION)
        scales.append(
            jnp.concatenate([jnp.broadcast_to(v, (1, 128)) for v in pair], axis=1)
        )
        factors.append(
            jnp.where(
                sub < 4,
                jnp.broadcast_to(UNIT / pair[0], (8, 128)),
                jnp.broadcast_to(UNIT / pair[1], (8, 128)),
            )
        )

    def quantize(m):
        factor = factors[m][None]

        def values(p, yh, yl):
            block = codes[p, yh, :, yl, :, m].reshape(zhs * 2, 8, 128)
            level = block.astype(jnp.int32).astype(jnp.float32)
            square = level * level
            q = square * square * level * factor
            return snap(jnp.clip(q, -SATURATION, SATURATION))

        def step(t, carry):
            y = t // xs
            x = t % xs
            even = values(2 * x, y // 2, y % 2)
            odd = values(2 * x + 1, y // 2, y % 2)
            first_half = (lax.broadcasted_iota(jnp.int32, even.shape, 1)) < 4
            left = jnp.where(first_half, even, pltpu.roll(odd, 4, 1))
            right = jnp.where(first_half, pltpu.roll(even, 4, 1), odd)
            rows = pl.ds(pl.multiple_of(t * 64, 64), 64)
            packed[m, rows, 0:128] = left.reshape(64, 128).astype(jnp.bfloat16)
            packed[m, rows, 128:256] = right.reshape(64, 128).astype(jnp.bfloat16)
            return carry

        lax.fori_loop(0, xs * yhs * 2, step, 0)

    for m in range(3):
        quantize(m)
    token_rows = tokens[...]
    gate_act = jnp.dot(token_rows, packed[0], preferred_element_type=jnp.float32) * scales[0]
    up_act = jnp.dot(token_rows, packed[1], preferred_element_type=jnp.float32) * scales[1]
    hidden = gate_act / (1.0 + jnp.exp(-gate_act)) * up_act * scales[2]
    partial_value = lax.dot_general(
        hidden.astype(jnp.bfloat16),
        packed[2],
        (((1,), (1,)), ((), ())),
        preferred_element_type=jnp.float32,
    )
    homes, lines = out.shape[1], out.shape[2]
    rows = partial_value.shape[0] // 4
    for r in range(4):
        for k in range(lines // CAP):
            spread[r, pl.ds(k, rows, lines // CAP), :] = partial_value[
                r * rows : (r + 1) * rows, k * 128 : (k + 1) * 128
            ]
        out[quarter[0] ^ r] = spread[r].reshape(homes, lines, 128).astype(jnp.bfloat16)


def experts(quarter, codes, tokens):
    rows, width = tokens.shape
    homes = rows // (4 * CAP)
    lines = CAP * width // 128
    vmem = pl.BlockSpec(memory_space=pltpu.VMEM)
    return pl.pallas_call(
        expert_kernel,
        out_shape=jax.ShapeDtypeStruct((4, homes, lines, 128), jnp.bfloat16),
        in_specs=[pl.BlockSpec(memory_space=pltpu.SMEM), vmem, vmem],
        out_specs=vmem,
        scratch_shapes=[
            pltpu.VMEM((3, width, 256), jnp.bfloat16),
            pltpu.VMEM((4, homes * lines, 128), jnp.float32),
        ],
        compiler_params=pltpu.CompilerParams(vmem_limit_bytes=40 * 2**20),
    )(quarter, codes, tokens)


def combine_kernel(returned, weighted, out, total):
    lines = returned.shape[2]
    width = lines // CAP
    rows = weighted.shape[0]
    weights = weighted[...]
    sums = [jnp.zeros((width, 128), jnp.float32) for _ in range(rows)]
    for e in range(returned.shape[1]):
        for j in range(CAP):
            value = jnp.zeros((width, 128), jnp.float32)
            for q in range(returned.shape[0]):
                value = value + returned[q, e, j * width : (j + 1) * width].astype(jnp.float32)
            for t in range(rows):
                slot = e * CAP + j
                sums[t] = sums[t] + weights[t : t + 1, slot : slot + 1] * value
    for t in range(rows):
        total[t * width : (t + 1) * width] = sums[t]
    for k in range(width):
        out[:, k * 128 : (k + 1) * 128] = total[pl.ds(k, rows, width), :].astype(jnp.bfloat16)


def combine(returned, weighted):
    rows = weighted.shape[0]
    width = returned.shape[2] // CAP
    vmem = pl.BlockSpec(memory_space=pltpu.VMEM)
    return pl.pallas_call(
        combine_kernel,
        out_shape=jax.ShapeDtypeStruct((rows, width * 128), jnp.bfloat16),
        in_specs=[vmem, vmem],
        out_specs=vmem,
        scratch_shapes=[pltpu.VMEM((rows * width, 128), jnp.float32)],
        compiler_params=pltpu.CompilerParams(vmem_limit_bytes=16 * 2**20),
    )(returned, weighted)


def body(master, moment_one, moment_two, gradient, states, norm_gain, routes, route_weights):
    owners = lax.axis_size(OWNERS)
    updated, codes = adam_update(master, moment_one, moment_two, gradient, owners)
    columns = lax.all_to_all(codes, OWNERS, split_axis=0, concat_axis=0, tiled=True)
    gathered_codes = lax.all_gather(columns, COPIES, axis=0, tiled=False)

    normed = rms_norm(states, norm_gain)
    weights = route_weights / jnp.sum(route_weights, axis=1, keepdims=True)
    row_count = routes.shape[0]
    group_size = owners // E
    expert_ids = routes.reshape(-1)
    onehot = (expert_ids[:, None] == jnp.arange(E, dtype=jnp.int32)[None, :]).astype(jnp.int32)
    earlier = jnp.cumsum(onehot, axis=0) - onehot
    slot_index = jnp.sum(earlier * onehot, axis=1)
    position = expert_ids * CAP + slot_index
    placed = (position[:, None] == jnp.arange(E * CAP, dtype=jnp.int32)[None, :]).astype(
        jnp.float32
    )
    placed = placed.reshape(row_count, TOP, E * CAP)
    select = jnp.sum(placed, axis=1).astype(jnp.bfloat16)
    weighted = jnp.sum(placed * weights[:, :, None], axis=1)
    gathered = lax.dot_general(
        select, normed, (((0,), (0,)), ((), ())), preferred_element_type=jnp.float32
    )
    width = normed.shape[1]
    buffer = gathered.astype(jnp.bfloat16).reshape(E, CAP, width)
    mine = lax.all_to_all(buffer, EXPERTS, split_axis=0, concat_axis=0, tiled=True)
    mine = mine.reshape(E * CAP, width)
    swap = [[(i, i ^ r) for i in range(4)] for r in range(4)]
    parts = [mine] + [lax.ppermute(mine, QUARTERS, swap[r]) for r in (1, 2, 3)]
    tokens = jnp.concatenate(parts)
    quarter = lax.axis_index(QUARTERS).astype(jnp.int32).reshape(1)

    copies = gathered_codes.shape[0]
    gathered_codes = gathered_codes.reshape(copies, 4, 4, 2, 2, 3, 8, 128)
    partial_value = experts(quarter, gathered_codes, tokens)
    lines = partial_value.shape[2]
    returned = lax.all_to_all(
        partial_value.reshape(owners, lines, 128), HOMES, split_axis=0, concat_axis=0, tiled=True
    )
    mixture = combine(returned.reshape(group_size, E, lines, 128), weighted)
    return (updated, mixture)


def solution(mesh):
    chips = Mesh(mesh.devices.reshape(4, 2, 4, 4, 2, 2), AXES)
    rows = P(None, AXES, None)
    return jax.shard_map(
        body,
        mesh=chips,
        in_specs=(rows, rows, rows, rows, P(AXES, None), P(), P(AXES, None), P(AXES, None)),
        out_specs=(rows, P(AXES, None)),
        check_vma=False,
    )
```

```python
import jax
import jax.numpy as jnp
from jax import lax
from jax.experimental import pallas as pl
from jax.experimental.pallas import tpu as pltpu
from jax.sharding import Mesh, PartitionSpec as P

E = 16
TOP = 8
QBLOCK = 128
STEP = 10
CAP = 3

BETA_ONE = 0.9
BETA_TWO = 0.95
LEARN_RATE = 0.01
ADAM_EPSILON = 1e-08
WEIGHT_DECAY = 0.1
SATURATION = 448.0
SCALE_EPSILON = 1e-06
NORM_EPSILON = 1e-06

BOUND = 0.1875
LEVELS = 32767.0
UNIT = BOUND / LEVELS**5

TOKEN_BOUND = 68.0
TOKEN_UNIT = TOKEN_BOUND / LEVELS**5

AXES = ("yh", "yl", "x", "zh", "zl", "c")
OWNERS = ("yh", "zh", "yl", "zl")
COPIES = ("x", "c")


def adam_tile(master, moment_one, moment_two, grad_float):
    first = BETA_ONE * moment_one + (1.0 - BETA_ONE) * grad_float
    second = BETA_TWO * moment_two + (1.0 - BETA_TWO) * grad_float * grad_float
    correct_one = 1.0 - BETA_ONE**STEP
    correct_two = 1.0 - BETA_TWO**STEP
    mean = second * (1.0 / correct_two)
    spread = mean * lax.rsqrt(mean) + ADAM_EPSILON
    inverse = pl.reciprocal(spread, approx=True)
    inverse = inverse * (2.0 - spread * inverse)
    direction = first * (1.0 / correct_one) * inverse
    return master - LEARN_RATE * (direction + WEIGHT_DECAY * master)


def encode(values, bound):
    magnitude = jnp.maximum(jnp.abs(values) * (1.0 / bound), 1e-30)
    level = jnp.minimum(jnp.exp2(jnp.log2(magnitude) * 0.2) * LEVELS + 0.5, LEVELS)
    return jnp.where(values < 0, -level, level).astype(jnp.int32)


def dispatch(states, norm_gain, routes, route_weights, weighted, lines, chosen):
    rows, width = states.shape
    blocks = width // 128
    values = states[...].astype(jnp.float32)
    mean_square = jnp.mean(values * values, axis=1, keepdims=True)
    normed = values * lax.rsqrt(mean_square + NORM_EPSILON) * norm_gain[...]
    level = encode(normed, TOKEN_BOUND).astype(jnp.float32)
    for k in range(blocks):
        lines[pl.ds(k, rows, blocks), :] = level[:, k * 128 : (k + 1) * 128]

    lane = lax.broadcasted_iota(jnp.int32, (rows, 128), 1)
    expert = lane // CAP
    ids = routes[...]
    gains = route_weights[...]
    gains = gains / jnp.sum(gains, axis=1, keepdims=True)
    named = jnp.zeros((rows, 128), jnp.float32)
    gain = jnp.zeros((rows, 128), jnp.float32)
    for k in range(TOP):
        hit = ids[:, k : k + 1] == expert
        named = jnp.where(hit, 1.0, named)
        gain = jnp.where(hit, gains[:, k : k + 1], gain)
    slot = (lane - expert * CAP).astype(jnp.float32)
    earlier = jnp.zeros((1, 128), jnp.float32)
    picks = []
    for t in range(rows):
        pick = jnp.where(earlier == slot[t : t + 1], named[t : t + 1], 0.0)
        weighted[t : t + 1, :] = pick * gain[t : t + 1]
        picks.append(pick)
        earlier = earlier + named[t : t + 1]
    tiles = [lines[t * blocks : (t + 1) * blocks] for t in range(rows)]
    for n in range(E * CAP):
        row = picks[0][:, n : n + 1] * tiles[0]
        for t in range(1, rows):
            row = row + picks[t][:, n : n + 1] * tiles[t]
        chosen[n] = row.astype(jnp.int32).astype(jnp.int16).reshape(2, 8, 128)


def owner_kernel(
    master, moment_one, moment_two, gradient, states, norm_gain, routes, route_weights,
    updated, codes, weighted, lines, chosen,
):
    step = pl.program_id(0)

    @pl.when(step == 0)
    def _():
        dispatch(states, norm_gain, routes, route_weights, weighted, lines, chosen)

    dests = codes.shape[0]
    for d in range(dests):
        left = slice(d * 256, d * 256 + 128)
        right = slice(d * 256 + 128, d * 256 + 256)
        for m in range(3):

            def tile(ref):
                return jnp.concatenate(
                    [ref[m, :, left].astype(jnp.float32), ref[m, :, right].astype(jnp.float32)],
                    axis=0,
                )

            value = adam_tile(tile(master), tile(moment_one), tile(moment_two), tile(gradient))
            updated[m, :, left] = value[0:4]
            updated[m, :, right] = value[4:8]
            codes[d, m] = encode(value, BOUND).astype(jnp.int16)
        for j in range(CAP):
            slot = (step * (dests // 4) + d // 4) * CAP + j
            codes[d, 3 + j] = chosen[slot, d % 2]


def prepare(master, moment_one, moment_two, gradient, states, norm_gain, routes, route_weights, owners):
    steps = 2
    columns = master.shape[2] // steps
    rows = pl.BlockSpec((3, 4, columns), lambda i: (0, 0, i))
    whole = lambda array: pl.BlockSpec(array.shape, lambda i: (0, 0))
    count, width = states.shape
    small = (states, norm_gain, routes, route_weights)
    return pl.pallas_call(
        owner_kernel,
        grid=(steps,),
        out_shape=(
            jax.ShapeDtypeStruct(master.shape, jnp.float32),
            jax.ShapeDtypeStruct((owners, 3 + CAP, 8, 128), jnp.int16),
            jax.ShapeDtypeStruct((count, 128), jnp.float32),
        ),
        in_specs=[rows] * 4 + [whole(array) for array in small],
        out_specs=(
            rows,
            pl.BlockSpec((owners // steps, 3 + CAP, 8, 128), lambda i: (i, 0, 0, 0)),
            pl.BlockSpec((count, 128), lambda i: (0, 0)),
        ),
        scratch_shapes=[
            pltpu.VMEM((count * width // 128, 128), jnp.float32),
            pltpu.VMEM((E * CAP, 2, 8, 128), jnp.int16),
        ],
        compiler_params=pltpu.CompilerParams(vmem_limit_bytes=60 * 2**20),
    )(master, moment_one, moment_two, gradient, *small)


def snap(q):
    clipped = jnp.clip(q, -SATURATION, SATURATION)
    return clipped.astype(jnp.float8_e4m3fn).astype(jnp.bfloat16)


def expert_kernel(place, codes, near, far, out, packed, spread, lines):
    copies = codes.shape[0]
    xs, yhs, zhs = copies // 2, codes.shape[1], codes.shape[2]

    def extremes(step, carry):
        high, low = carry
        p = step // yhs
        yh = step % yhs
        block = codes[p, yh].astype(jnp.int32).reshape(zhs * 4, 3, 8, 128)
        return jnp.maximum(high, jnp.max(block, axis=0)), jnp.minimum(low, jnp.min(block, axis=0))

    zero = jnp.zeros((3, 8, 128), jnp.int32)
    high, low = lax.fori_loop(0, copies * yhs, extremes, (zero, zero), unroll=4)
    top = jnp.maximum(high, -low).astype(jnp.float32)
    sub = lax.broadcasted_iota(jnp.int32, (8, 128), 0)
    scales = []
    factors = []
    for m in range(3):
        pair = []
        for h in range(2):
            level = jnp.max(
                jnp.max(top[m, 4 * h : 4 * h + 4], axis=0, keepdims=True), axis=1, keepdims=True
            )
            square = level * level
            largest = square * square * level * UNIT
            pair.append((largest + SCALE_EPSILON) / SATURATION)
        scales.append(
            jnp.concatenate([jnp.broadcast_to(v, (1, 128)) for v in pair], axis=1)
        )
        factors.append(
            jnp.where(
                sub < 4,
                jnp.broadcast_to(UNIT / pair[0], (8, 128)),
                jnp.broadcast_to(UNIT / pair[1], (8, 128)),
            )
        )

    def quantize(m):
        factor = factors[m][None]

        def values(p, yh, yl):
            block = codes[p, yh, :, yl, :, m].reshape(zhs * 2, 8, 128)
            level = block.astype(jnp.int32).astype(jnp.float32)
            square = level * level
            q = square * square * level * factor
            return q

        def step(t, carry):
            y = t // xs
            x = t % xs
            even = values(2 * x, y // 2, y % 2)
            odd = values(2 * x + 1, y // 2, y % 2)
            first_half = (lax.broadcasted_iota(jnp.int32, even.shape, 1)) < 4
            left = jnp.where(first_half, even, pltpu.roll(odd, 4, 1))
            right = jnp.where(first_half, pltpu.roll(even, 4, 1), odd)
            rows = pl.ds(pl.multiple_of(t * 64, 64), 64)
            packed[m, rows, 0:128] = snap(left.reshape(64, 128))
            packed[m, rows, 128:256] = snap(right.reshape(64, 128))
            return carry

        lax.fori_loop(0, xs * yhs * 2, step, 0, unroll=4)

    for m in range(3):
        quantize(m)
    gate_act = jnp.zeros((lines.shape[0] // 8, 256), jnp.float32)
    up_act = jnp.zeros((lines.shape[0] // 8, 256), jnp.float32)
    half = packed.shape[1] // 2
    for part, own in ((near, place[0]), (far, 1 - place[0])):
        level = part[...].astype(jnp.int32).astype(jnp.float32)
        square = level * level
        lines[...] = (square * square * level * TOKEN_UNIT).reshape(lines.shape)
        token_rows = jnp.concatenate(
            [lines[pl.ds(k, lines.shape[0] // 8, 8), :].astype(jnp.bfloat16) for k in range(8)], axis=1
        )
        features = pl.ds(pl.multiple_of(own * half, half), half)
        gate_act += jnp.dot(token_rows, packed[0, features], preferred_element_type=jnp.float32)
        up_act += jnp.dot(token_rows, packed[1, features], preferred_element_type=jnp.float32)
    gate_act = gate_act * scales[0]
    up_act = up_act * scales[1]
    hidden = gate_act / (1.0 + jnp.exp(-gate_act)) * up_act * scales[2]
    partial_value = lax.dot_general(
        hidden.astype(jnp.bfloat16),
        packed[2],
        (((1,), (1,)), ((), ())),
        preferred_element_type=jnp.float32,
    )
    rows = partial_value.shape[0]
    for k in range(out.shape[1] // CAP):
        spread[pl.ds(k, rows, out.shape[1] // CAP), :] = partial_value[:, k * 128 : (k + 1) * 128]
    out[...] = spread[...].reshape(out.shape).astype(jnp.bfloat16)


def experts(place, codes, near, far):
    sources = near.shape[0]
    width = 2 * 8 * 128
    lines = CAP * width // 128
    vmem = pl.BlockSpec(memory_space=pltpu.VMEM)
    return pl.pallas_call(
        expert_kernel,
        out_shape=jax.ShapeDtypeStruct((sources, lines, 128), jnp.bfloat16),
        in_specs=[pl.BlockSpec(memory_space=pltpu.SMEM), vmem, vmem, vmem],
        out_specs=vmem,
        scratch_shapes=[
            pltpu.VMEM((3, width, 256), jnp.bfloat16),
            pltpu.VMEM((sources * lines, 128), jnp.float32),
            pltpu.VMEM((sources * CAP * 8, 128), jnp.float32),
        ],
        compiler_params=pltpu.CompilerParams(vmem_limit_bytes=40 * 2**20),
    )(place, codes, near, far)


def combine_kernel(returned, weighted, out, total):
    lines = returned.shape[2]
    width = lines // CAP
    rows = weighted.shape[0]
    weights = weighted[...]
    sums = [jnp.zeros((width, 128), jnp.float32) for _ in range(rows)]
    for e in range(returned.shape[0]):
        for j in range(CAP):
            value = jnp.zeros((width, 128), jnp.float32)
            for q in range(returned.shape[1]):
                value = value + returned[e, q, j * width : (j + 1) * width].astype(jnp.float32)
            for t in range(rows):
                slot = e * CAP + j
                sums[t] = sums[t] + weights[t : t + 1, slot : slot + 1] * value
    for t in range(rows):
        total[t * width : (t + 1) * width] = sums[t]
    for k in range(width):
        out[:, k * 128 : (k + 1) * 128] = total[pl.ds(k, rows, width), :].astype(jnp.bfloat16)


def combine(returned, weighted):
    rows = weighted.shape[0]
    width = returned.shape[2] // CAP
    vmem = pl.BlockSpec(memory_space=pltpu.VMEM)
    return pl.pallas_call(
        combine_kernel,
        out_shape=jax.ShapeDtypeStruct((rows, width * 128), jnp.bfloat16),
        in_specs=[vmem, vmem],
        out_specs=vmem,
        scratch_shapes=[pltpu.VMEM((rows * width, 128), jnp.float32)],
        compiler_params=pltpu.CompilerParams(vmem_limit_bytes=16 * 2**20),
    )(returned, weighted)


def body(master, moment_one, moment_two, gradient, states, norm_gain, routes, route_weights):
    owners = lax.axis_size(OWNERS)
    updated, codes, weighted = prepare(
        master, moment_one, moment_two, gradient, states, norm_gain[None, :], routes, route_weights, owners
    )
    received = lax.all_to_all(codes, OWNERS, split_axis=0, concat_axis=0, tiled=True)
    near = received[:, 3:]
    far = lax.ppermute(near, "zl", [(0, 1), (1, 0)])
    gathered = lax.all_gather(received[:, :3], COPIES, axis=0, tiled=False)
    place = lax.axis_index("zl").astype(jnp.int32).reshape(1)
    partial_value = experts(place, gathered.reshape(-1, 4, 4, 2, 2, 3, 8, 128), near, far)
    returned = lax.all_to_all(partial_value, OWNERS, split_axis=0, concat_axis=0, tiled=True)
    mixture = combine(returned.reshape(E, owners // E, -1, 128), weighted)
    return (updated, mixture)


def solution(mesh):
    chips = Mesh(mesh.devices.reshape(4, 2, 4, 4, 2, 2), AXES)
    rows = P(None, AXES, None)
    return jax.shard_map(
        body,
        mesh=chips,
        in_specs=(rows, rows, rows, rows, P(AXES, None), P(), P(AXES, None), P(AXES, None)),
        out_specs=(rows, P(AXES, None)),
        check_vma=False,
    )
```

```python
import jax
import jax.numpy as jnp
from jax import lax
from jax.experimental import pallas as pl
from jax.experimental.pallas import tpu as pltpu
from jax.sharding import Mesh, PartitionSpec as P

E = 16
TOP = 8
QBLOCK = 128
STEP = 10
CAP = 3

BETA_ONE = 0.9
BETA_TWO = 0.95
LEARN_RATE = 0.01
ADAM_EPSILON = 1e-08
WEIGHT_DECAY = 0.1
SATURATION = 448.0
SCALE_EPSILON = 1e-06
NORM_EPSILON = 1e-06

BOUND = 0.1875
LEVELS = 32767.0
UNIT = BOUND / LEVELS**5

TOKEN_BOUND = 68.0
TOKEN_UNIT = TOKEN_BOUND / LEVELS**5
ACT_BOUND = 524288.0
ACT_UNIT = ACT_BOUND / LEVELS**7

AXES = ("yh", "yl", "x", "zh", "zl", "c")
OWNERS = ("yh", "zh", "yl", "zl")
COPIES = ("x", "c")


def adam_tile(master, moment_one, moment_two, grad_float):
    first = BETA_ONE * moment_one + (1.0 - BETA_ONE) * grad_float
    second = BETA_TWO * moment_two + (1.0 - BETA_TWO) * grad_float * grad_float
    correct_one = 1.0 - BETA_ONE**STEP
    correct_two = 1.0 - BETA_TWO**STEP
    mean = second * (1.0 / correct_two)
    spread = mean * lax.rsqrt(mean) + ADAM_EPSILON
    inverse = pl.reciprocal(spread, approx=True)
    inverse = inverse * (2.0 - spread * inverse)
    direction = first * (1.0 / correct_one) * inverse
    return master - LEARN_RATE * (direction + WEIGHT_DECAY * master)


def encode(values, bound, power=5):
    magnitude = jnp.maximum(jnp.abs(values) * (1.0 / bound), 1e-35)
    level = jnp.minimum(jnp.exp2(jnp.log2(magnitude) * (1.0 / power)) * LEVELS + 0.5, LEVELS)
    return jnp.where(values < 0, -level, level).astype(jnp.int32)


def dispatch(states, norm_gain, routes, route_weights, weighted, lines, chosen):
    rows, width = states.shape
    blocks = width // 128
    values = states[...].astype(jnp.float32)
    mean_square = jnp.mean(values * values, axis=1, keepdims=True)
    normed = values * lax.rsqrt(mean_square + NORM_EPSILON) * norm_gain[...]
    level = encode(normed, TOKEN_BOUND).astype(jnp.float32)
    for k in range(blocks):
        lines[pl.ds(k, rows, blocks), :] = level[:, k * 128 : (k + 1) * 128]

    lane = lax.broadcasted_iota(jnp.int32, (rows, 128), 1)
    expert = lane // CAP
    ids = routes[...]
    gains = route_weights[...]
    gains = gains / jnp.sum(gains, axis=1, keepdims=True)
    named = jnp.zeros((rows, 128), jnp.float32)
    gain = jnp.zeros((rows, 128), jnp.float32)
    for k in range(TOP):
        hit = ids[:, k : k + 1] == expert
        named = jnp.where(hit, 1.0, named)
        gain = jnp.where(hit, gains[:, k : k + 1], gain)
    slot = (lane - expert * CAP).astype(jnp.float32)
    earlier = jnp.zeros((1, 128), jnp.float32)
    picks = []
    for t in range(rows):
        pick = jnp.where(earlier == slot[t : t + 1], named[t : t + 1], 0.0)
        weighted[t : t + 1, :] = pick * gain[t : t + 1]
        picks.append(pick)
        earlier = earlier + named[t : t + 1]
    tiles = [lines[t * blocks : (t + 1) * blocks] for t in range(rows)]
    for n in range(E * CAP):
        row = picks[0][:, n : n + 1] * tiles[0]
        for t in range(1, rows):
            row = row + picks[t][:, n : n + 1] * tiles[t]
        chosen[n] = row.astype(jnp.int32).astype(jnp.int16).reshape(2, 8, 128)


def owner_kernel(
    master, moment_one, moment_two, gradient, states, norm_gain, routes, route_weights,
    updated, codes, weighted, lines, chosen,
):
    step = pl.program_id(0)

    @pl.when(step == 0)
    def _():
        dispatch(states, norm_gain, routes, route_weights, weighted, lines, chosen)

    dests = codes.shape[0]
    pair_rows = lax.broadcasted_iota(jnp.int32, (8, 128), 0) % 4 < 2
    down = []
    for d in range(dests):
        left = slice(d * 256, d * 256 + 128)
        right = slice(d * 256 + 128, d * 256 + 256)
        for m in range(3):

            def tile(ref):
                return jnp.concatenate(
                    [ref[m, :, left].astype(jnp.float32), ref[m, :, right].astype(jnp.float32)],
                    axis=0,
                )

            value = adam_tile(tile(master), tile(moment_one), tile(moment_two), tile(gradient))
            updated[m, :, left] = value[0:4]
            updated[m, :, right] = value[4:8]
            if m < 2:
                codes[d, m] = encode(value, BOUND).astype(jnp.int16)
            else:
                down.append(encode(value, BOUND))
        if d % 2:
            first, second = down[d - 1], down[d]
            low = jnp.where(pair_rows, first, pltpu.roll(second, 2, 0))
            high = jnp.where(pair_rows, pltpu.roll(first, 6, 0), second)
            codes[d - 1, 2] = low.astype(jnp.int16)
            codes[d, 2] = high.astype(jnp.int16)
        for j in range(CAP):
            slot = (step * (dests // 4) + d // 4) * CAP + j
            codes[d, 3 + j] = chosen[slot, d % 2]


def prepare(master, moment_one, moment_two, gradient, states, norm_gain, routes, route_weights, owners):
    steps = 2
    columns = master.shape[2] // steps
    rows = pl.BlockSpec((3, 4, columns), lambda i: (0, 0, i))
    whole = lambda array: pl.BlockSpec(array.shape, lambda i: (0, 0))
    count, width = states.shape
    small = (states, norm_gain, routes, route_weights)
    return pl.pallas_call(
        owner_kernel,
        grid=(steps,),
        out_shape=(
            jax.ShapeDtypeStruct(master.shape, jnp.float32),
            jax.ShapeDtypeStruct((owners, 3 + CAP, 8, 128), jnp.int16),
            jax.ShapeDtypeStruct((count, 128), jnp.float32),
        ),
        in_specs=[rows] * 4 + [whole(array) for array in small],
        out_specs=(
            rows,
            pl.BlockSpec((owners // steps, 3 + CAP, 8, 128), lambda i: (i, 0, 0, 0)),
            pl.BlockSpec((count, 128), lambda i: (0, 0)),
        ),
        scratch_shapes=[
            pltpu.VMEM((count * width // 128, 128), jnp.float32),
            pltpu.VMEM((E * CAP, 2, 8, 128), jnp.int16),
        ],
        compiler_params=pltpu.CompilerParams(vmem_limit_bytes=60 * 2**20),
    )(master, moment_one, moment_two, gradient, *small)


def snap(q):
    clipped = jnp.clip(q, -SATURATION, SATURATION)
    return clipped.astype(jnp.float8_e4m3fn).astype(jnp.bfloat16)


def level_value(level, unit):
    square = level * level
    return square * square * level * unit


def block_level(top, rows):
    return jnp.max(jnp.max(top[rows], axis=0, keepdims=True), axis=1, keepdims=True)


def scale_of(level):
    return (level_value(level, UNIT) + SCALE_EPSILON) / SATURATION


def gate_kernel(place, codes, near, far, out, packed, lines):
    copies = codes.shape[0]
    xs, yhs, zhs = copies // 2, codes.shape[1], codes.shape[2]
    rows = near.shape[0] * CAP

    def extremes(step, carry):
        high, low = carry
        p = step // yhs
        yh = step % yhs
        block = codes[p, yh].astype(jnp.int32).reshape(zhs * 4, 3, 8, 128)
        return jnp.maximum(high, jnp.max(block, axis=0)), jnp.minimum(low, jnp.min(block, axis=0))

    zero = jnp.zeros((3, 8, 128), jnp.int32)
    high, low = lax.fori_loop(0, copies * yhs, extremes, (zero, zero), unroll=4)
    top = jnp.maximum(high, -low).astype(jnp.float32)
    sub = lax.broadcasted_iota(jnp.int32, (8, 128), 0)
    scales = []
    factors = []
    for m in range(2):
        pair = [scale_of(block_level(top[m], slice(4 * h, 4 * h + 4))) for h in range(2)]
        scales.append(jnp.concatenate([jnp.broadcast_to(v, (1, 128)) for v in pair], axis=1))
        wide = [jnp.broadcast_to(UNIT / v, (8, 128)) for v in pair]
        factors.append(jnp.where(sub < 4, wide[0], wide[1]))

    def quantize(m):
        factor = factors[m][None]

        def values(p, yh, yl):
            block = codes[p, yh, :, yl, :, m].reshape(zhs * 2, 8, 128)
            return level_value(block.astype(jnp.int32).astype(jnp.float32), factor)

        def step(t, carry):
            y = t // xs
            x = t % xs
            even = values(2 * x, y // 2, y % 2)
            odd = values(2 * x + 1, y // 2, y % 2)
            first_half = (lax.broadcasted_iota(jnp.int32, even.shape, 1)) < 4
            left = jnp.where(first_half, even, pltpu.roll(odd, 4, 1))
            right = jnp.where(first_half, pltpu.roll(even, 4, 1), odd)
            span = pl.ds(pl.multiple_of(t * 64, 64), 64)
            packed[m, span, 0:128] = snap(left.reshape(64, 128))
            packed[m, span, 128:256] = snap(right.reshape(64, 128))
            return carry

        lax.fori_loop(0, xs * yhs * 2, step, 0, unroll=4)

    for m in range(2):
        quantize(m)
    gate_act = jnp.zeros((rows, 256), jnp.float32)
    up_act = jnp.zeros((rows, 256), jnp.float32)
    half = packed.shape[1] // 2
    for part, own in ((near, place[0]), (far, 1 - place[0])):
        level = part[...].astype(jnp.int32).astype(jnp.float32)
        lines[...] = level_value(level, TOKEN_UNIT).reshape(lines.shape)
        token_rows = jnp.concatenate(
            [lines[pl.ds(k, rows, 8), :].astype(jnp.bfloat16) for k in range(8)], axis=1
        )
        features = pl.ds(pl.multiple_of(own * half, half), half)
        gate_act += jnp.dot(token_rows, packed[0, features], preferred_element_type=jnp.float32)
        up_act += jnp.dot(token_rows, packed[1, features], preferred_element_type=jnp.float32)
    gate_act = gate_act * scales[0]
    up_act = up_act * scales[1]
    act = gate_act / (1.0 + jnp.exp(-gate_act)) * up_act
    out[0:rows] = encode(act, ACT_BOUND, 7).astype(jnp.int16)
    levels = [block_level(top[2], slice(2 * b, 2 * b + 2)) for b in range(4)]
    line = jnp.concatenate([jnp.broadcast_to(v, (16, 64)) for v in levels], axis=1)
    out[rows : rows + 16] = line.astype(jnp.int32).astype(jnp.int16)


def gate_up(place, codes, near, far):
    sources = near.shape[0]
    width = 2 * 8 * 128
    vmem = pl.BlockSpec(memory_space=pltpu.VMEM)
    return pl.pallas_call(
        gate_kernel,
        out_shape=jax.ShapeDtypeStruct((sources * CAP + 16, 256), jnp.int16),
        in_specs=[pl.BlockSpec(memory_space=pltpu.SMEM), vmem, vmem, vmem],
        out_specs=vmem,
        scratch_shapes=[
            pltpu.VMEM((2, width, 256), jnp.bfloat16),
            pltpu.VMEM((sources * CAP * 8, 128), jnp.float32),
        ],
        compiler_params=pltpu.CompilerParams(vmem_limit_bytes=20 * 2**20),
    )(place, codes, near, far)


def down_kernel(codes, acts, out, packed, spread):
    copies = codes.shape[0]
    xs, yhs, zhs = copies // 2, codes.shape[1], codes.shape[2]
    rows = acts.shape[1] - 16
    sub = lax.broadcasted_iota(jnp.int32, (8, 128), 0)
    marks = acts[:, rows : rows + 16].astype(jnp.int32).astype(jnp.float32)
    line = jnp.max(jnp.maximum(marks[0], marks[1]), axis=0, keepdims=True)
    level = acts[:, 0:rows].astype(jnp.int32).astype(jnp.float32)
    square = level * level
    act = (square * square * square * level * ACT_UNIT).astype(jnp.bfloat16)
    scales = [None] * 4
    factor = jnp.zeros((8, 128), jnp.float32)
    for h in range(2):
        for t in range(2):
            b = 2 * h + t
            scale = scale_of(jnp.max(line[:, b * 64 : (b + 1) * 64], axis=1, keepdims=True))
            scales[2 * t + h] = scale
            factor = jnp.where(sub // 2 == b, jnp.broadcast_to(UNIT / scale, (8, 128)), factor)
    factor = factor[None]
    low_pair = (lax.broadcasted_iota(jnp.int32, (zhs, 8, 128), 1)) % 4 < 2
    low_half = (lax.broadcasted_iota(jnp.int32, (zhs, 8, 128), 1)) < 4

    def values(p, yh, yl, zl):
        block = codes[p, yh, :, yl, zl, 2]
        return level_value(block.astype(jnp.int32).astype(jnp.float32), factor)

    def step(i, carry):
        y = i // xs
        x = i % xs
        yh, yl = y // 2, y % 2
        by_t = []
        for zl in range(2):
            even = values(2 * x, yh, yl, zl)
            odd = values(2 * x + 1, yh, yl, zl)
            by_t.append(
                (
                    jnp.where(low_pair, even, pltpu.roll(odd, 2, 1)),
                    jnp.where(low_pair, pltpu.roll(even, 6, 1), odd),
                )
            )
        span = pl.ds(pl.multiple_of(i * zhs * 8, zhs * 8), zhs * 8)
        for t in range(2):
            near, far = by_t[0][t], by_t[1][t]
            top = jnp.where(low_half, near, pltpu.roll(far, 4, 1))
            bottom = jnp.where(low_half, pltpu.roll(near, 4, 1), far)
            packed[span, 256 * t : 256 * t + 128] = snap(top.reshape(zhs * 8, 128))
            packed[span, 256 * t + 128 : 256 * t + 256] = snap(bottom.reshape(zhs * 8, 128))
        return carry

    lax.fori_loop(0, xs * yhs * 2, step, 0, unroll=4)
    partial_value = jnp.zeros((rows, packed.shape[0]), jnp.float32)
    for b in range(4):
        partial_value += scales[b] * lax.dot_general(
            act[b // 2, :, 128 * (b % 2) : 128 * (b % 2) + 128],
            packed[:, 128 * b : 128 * b + 128],
            (((1,), (1,)), ((), ())),
            preferred_element_type=jnp.float32,
        )
    blocks = out.shape[1] // CAP
    for k in range(blocks):
        spread[pl.ds(k, rows, blocks), :] = partial_value[:, k * 128 : (k + 1) * 128]
    out[...] = spread[...].reshape(out.shape).astype(jnp.bfloat16)


def down(codes, acts):
    sources = (acts.shape[1] - 16) // CAP
    lines = CAP * 8
    vmem = pl.BlockSpec(memory_space=pltpu.VMEM)
    return pl.pallas_call(
        down_kernel,
        out_shape=jax.ShapeDtypeStruct((sources, lines, 128), jnp.bfloat16),
        in_specs=[vmem, vmem],
        out_specs=vmem,
        scratch_shapes=[
            pltpu.VMEM((lines // CAP * 128, 512), jnp.bfloat16),
            pltpu.VMEM((sources * lines, 128), jnp.float32),
        ],
        compiler_params=pltpu.CompilerParams(vmem_limit_bytes=20 * 2**20),
    )(codes, acts)


def combine_kernel(returned, weighted, out, total):
    experts, lines = returned.shape[0], returned.shape[3]
    width = lines // CAP
    rows = weighted.shape[0]
    weights = weighted[...]
    sums = [[jnp.zeros((width, 128), jnp.float32) for _ in range(rows)] for _ in range(2)]
    for e in range(experts):
        for j in range(CAP):
            slot = e * CAP + j
            for zl in range(2):
                value = returned[e, 0, zl, j * width : (j + 1) * width].astype(jnp.float32)
                value = value + returned[e, 1, zl, j * width : (j + 1) * width].astype(jnp.float32)
                for t in range(rows):
                    sums[zl][t] = sums[zl][t] + weights[t : t + 1, slot : slot + 1] * value
    source = lax.broadcasted_iota(jnp.int32, (128, 256), 0)
    target = lax.broadcasted_iota(jnp.int32, (128, 256), 1)
    placed = jnp.zeros((rows * width, 256), jnp.float32)
    for zl in range(2):
        spot = (target == source // 2 * 4 + 2 * zl + source % 2).astype(jnp.float32).astype(jnp.bfloat16)
        halves = jnp.concatenate(sums[zl], axis=0).astype(jnp.bfloat16)
        placed += jnp.dot(halves, spot, preferred_element_type=jnp.float32)
    total[0] = placed[:, 0:128]
    total[1] = placed[:, 128:256]
    for k in range(width):
        for h in range(2):
            out[:, k * 256 + h * 128 : k * 256 + h * 128 + 128] = total[
                h, pl.ds(k, rows, width), :
            ].astype(jnp.bfloat16)


def combine(returned, weighted):
    rows = weighted.shape[0]
    width = returned.shape[3] // CAP
    vmem = pl.BlockSpec(memory_space=pltpu.VMEM)
    return pl.pallas_call(
        combine_kernel,
        out_shape=jax.ShapeDtypeStruct((rows, width * 256), jnp.bfloat16),
        in_specs=[vmem, vmem],
        out_specs=vmem,
        scratch_shapes=[pltpu.VMEM((2, rows * width, 128), jnp.float32)],
        compiler_params=pltpu.CompilerParams(vmem_limit_bytes=16 * 2**20),
    )(returned, weighted)


def body(master, moment_one, moment_two, gradient, states, norm_gain, routes, route_weights):
    owners = lax.axis_size(OWNERS)
    updated, codes, weighted = prepare(
        master, moment_one, moment_two, gradient, states, norm_gain[None, :], routes, route_weights, owners
    )
    received = lax.all_to_all(codes, OWNERS, split_axis=0, concat_axis=0, tiled=True)
    near = received[:, 3:]
    far = lax.ppermute(near, "zl", [(0, 1), (1, 0)])
    gathered = lax.all_gather(received[:, :3], COPIES, axis=0, tiled=False)
    place = lax.axis_index("zl").astype(jnp.int32).reshape(1)
    gathered = gathered.reshape(-1, 4, 4, 2, 2, 3, 8, 128)
    acts = lax.all_gather(gate_up(place, gathered, near, far), "zl", axis=0, tiled=False)
    partial_value = down(gathered, acts)
    returned = lax.all_to_all(partial_value, OWNERS, split_axis=0, concat_axis=0, tiled=True)
    mixture = combine(returned.reshape(E, 2, 2, -1, 128), weighted)
    return (updated, mixture)


def solution(mesh):
    chips = Mesh(mesh.devices.reshape(4, 2, 4, 4, 2, 2), AXES)
    rows = P(None, AXES, None)
    return jax.shard_map(
        body,
        mesh=chips,
        in_specs=(rows, rows, rows, rows, P(AXES, None), P(), P(AXES, None), P(AXES, None)),
        out_specs=(rows, P(AXES, None)),
        check_vma=False,
    )
```

```python
import jax
import jax.numpy as jnp
from jax import lax
from jax.experimental import pallas as pl
from jax.experimental.pallas import tpu as pltpu
from jax.sharding import Mesh, PartitionSpec as P

E = 16
TOP = 8
QBLOCK = 128
STEP = 10
CAP = 3

BETA_ONE = 0.9
BETA_TWO = 0.95
LEARN_RATE = 0.01
ADAM_EPSILON = 1e-08
WEIGHT_DECAY = 0.1
SATURATION = 448.0
SCALE_EPSILON = 1e-06
NORM_EPSILON = 1e-06

BOUND = 0.1875
LEVELS = 32767.0
UNIT = BOUND / LEVELS**5

TOKEN_BOUND = 68.0
TOKEN_UNIT = TOKEN_BOUND / LEVELS**5
ACT_BOUND = 524288.0
ACT_UNIT = ACT_BOUND / LEVELS**7

AXES = ("yh", "yl", "x", "zh", "zl", "c")
OWNERS = ("yh", "zh", "yl", "zl")
COPIES = ("x", "c")


def adam_tile(master, moment_one, moment_two, grad_float):
    correct_one = LEARN_RATE / (1.0 - BETA_ONE**STEP)
    correct_two = 1.0 / (1.0 - BETA_TWO**STEP)
    first = (BETA_ONE * correct_one) * moment_one + ((1.0 - BETA_ONE) * correct_one) * grad_float
    second = (BETA_TWO * correct_two) * moment_two + (
        ((1.0 - BETA_TWO) * correct_two) * grad_float * grad_float
    )
    spread = second * lax.rsqrt(second) + ADAM_EPSILON
    inverse = pl.reciprocal(spread, approx=True)
    inverse = inverse * (2.0 - spread * inverse)
    return (1.0 - LEARN_RATE * WEIGHT_DECAY) * master - first * inverse


def encode(values, bound, power=5):
    magnitude = jnp.maximum(jnp.abs(values) * (1.0 / bound), 1e-35)
    level = jnp.minimum(jnp.exp2(jnp.log2(magnitude) * (1.0 / power)) * LEVELS + 0.5, LEVELS)
    return jnp.where(values < 0, -level, level).astype(jnp.int32)


def dispatch(states, norm_gain, routes, route_weights, weighted, lines, chosen):
    rows, width = states.shape
    blocks = width // 128
    values = states[...].astype(jnp.float32)
    mean_square = jnp.mean(values * values, axis=1, keepdims=True)
    normed = values * lax.rsqrt(mean_square + NORM_EPSILON) * norm_gain[...]
    level = encode(normed, TOKEN_BOUND).astype(jnp.float32)
    for k in range(blocks):
        lines[pl.ds(k, rows, blocks), :] = level[:, k * 128 : (k + 1) * 128]

    lane = lax.broadcasted_iota(jnp.int32, (rows, 128), 1)
    expert = lane // CAP
    ids = routes[...]
    gains = route_weights[...]
    gains = gains / jnp.sum(gains, axis=1, keepdims=True)
    named = jnp.zeros((rows, 128), jnp.float32)
    gain = jnp.zeros((rows, 128), jnp.float32)
    for k in range(TOP):
        hit = ids[:, k : k + 1] == expert
        named = jnp.where(hit, 1.0, named)
        gain = jnp.where(hit, gains[:, k : k + 1], gain)
    slot = (lane - expert * CAP).astype(jnp.float32)
    earlier = jnp.zeros((1, 128), jnp.float32)
    picks = []
    for t in range(rows):
        pick = jnp.where(earlier == slot[t : t + 1], named[t : t + 1], 0.0)
        weighted[t : t + 1, :] = pick * gain[t : t + 1]
        picks.append(pick)
        earlier = earlier + named[t : t + 1]
    tiles = [lines[t * blocks : (t + 1) * blocks] for t in range(rows)]
    for n in range(E * CAP):
        row = picks[0][:, n : n + 1] * tiles[0]
        for t in range(1, rows):
            row = row + picks[t][:, n : n + 1] * tiles[t]
        chosen[n] = row.astype(jnp.int32).astype(jnp.int16).reshape(2, 8, 128)


def owner_kernel(
    master, moment_one, moment_two, gradient, states, norm_gain, routes, route_weights,
    updated, codes, weighted, lines, chosen,
):
    step = pl.program_id(0)

    @pl.when(step == 0)
    def _():
        dispatch(states, norm_gain, routes, route_weights, weighted, lines, chosen)

    pair_rows = lax.broadcasted_iota(jnp.int32, (8, 128), 0) % 4 < 2
    group = 8

    def some(i, carry):
        down = []
        for d in range(group):
            owner = i * group + d
            for m in range(3):
                value = adam_tile(
                    master[m, owner], moment_one[m, owner], moment_two[m, owner],
                    gradient[m, owner].astype(jnp.float32),
                )
                updated[m, owner] = value
                if m < 2:
                    codes[owner, m] = encode(value, BOUND).astype(jnp.int16)
                else:
                    down.append(encode(value, BOUND))
            if d % 2:
                first, second = down[d - 1], down[d]
                low = jnp.where(pair_rows, first, pltpu.roll(second, 2, 0))
                high = jnp.where(pair_rows, pltpu.roll(first, 6, 0), second)
                codes[owner - 1, 2] = low.astype(jnp.int16)
                codes[owner, 2] = high.astype(jnp.int16)
            slot = (step * (codes.shape[0] // 4) + i * (group // 4) + d // 4) * CAP
            for j in range(CAP):
                codes[owner, 3 + j] = chosen[slot + j, d % 2]
        return carry

    lax.fori_loop(0, codes.shape[0] // group, some, 0)


def prepare(master, moment_one, moment_two, gradient, states, norm_gain, routes, route_weights, owners):
    steps = 2
    rows = pl.BlockSpec((3, owners // steps, 8, 128), lambda i: (0, i, 0, 0))
    whole = lambda array: pl.BlockSpec(array.shape, lambda i: (0, 0))
    count, width = states.shape
    small = (states, norm_gain, routes, route_weights)
    return pl.pallas_call(
        owner_kernel,
        grid=(steps,),
        out_shape=(
            jax.ShapeDtypeStruct(master.shape, jnp.float32),
            jax.ShapeDtypeStruct((owners, 3 + CAP, 8, 128), jnp.int16),
            jax.ShapeDtypeStruct((count, 128), jnp.float32),
        ),
        in_specs=[rows] * 4 + [whole(array) for array in small],
        out_specs=(
            rows,
            pl.BlockSpec((owners // steps, 3 + CAP, 8, 128), lambda i: (i, 0, 0, 0)),
            pl.BlockSpec((count, 128), lambda i: (0, 0)),
        ),
        scratch_shapes=[
            pltpu.VMEM((count * width // 128, 128), jnp.float32),
            pltpu.VMEM((E * CAP, 2, 8, 128), jnp.int16),
        ],
        compiler_params=pltpu.CompilerParams(vmem_limit_bytes=60 * 2**20),
    )(master, moment_one, moment_two, gradient, *small)


def to_tiles(array):
    matrices, rows, columns = array.shape
    parts = array.reshape(matrices, rows, columns // 256, 2, 128).transpose(0, 2, 3, 1, 4)
    return parts.reshape(matrices, columns // 256, 2 * rows, 128)


def from_tiles(tiles):
    matrices, owners = tiles.shape[:2]
    parts = tiles.reshape(matrices, owners, 2, 4, 128).transpose(0, 3, 1, 2, 4)
    return parts.reshape(matrices, 4, owners * 256)


def snap(q):
    clipped = jnp.clip(q, -SATURATION, SATURATION)
    return clipped.astype(jnp.float8_e4m3fn).astype(jnp.bfloat16)


def level_value(level, unit):
    square = level * level
    return square * square * level * unit


def block_level(top, rows):
    return jnp.max(jnp.max(top[rows], axis=0, keepdims=True), axis=1, keepdims=True)


def scale_of(level):
    return (level_value(level, UNIT) + SCALE_EPSILON) / SATURATION


def gate_kernel(place, codes, near, far, out, packed, lines):
    copies = codes.shape[0]
    xs, yhs, zhs = copies // 2, codes.shape[1], codes.shape[2]
    rows = near.shape[0] * CAP

    def extremes(step, carry):
        high, low = carry
        p = step // yhs
        yh = step % yhs
        block = codes[p, yh].astype(jnp.int32).reshape(zhs * 4, 3, 8, 128)
        return jnp.maximum(high, jnp.max(block, axis=0)), jnp.minimum(low, jnp.min(block, axis=0))

    zero = jnp.zeros((3, 8, 128), jnp.int32)
    high, low = lax.fori_loop(0, copies * yhs, extremes, (zero, zero), unroll=4)
    top = jnp.maximum(high, -low).astype(jnp.float32)
    sub = lax.broadcasted_iota(jnp.int32, (8, 128), 0)
    scales = []
    factors = []
    for m in range(2):
        pair = [scale_of(block_level(top[m], slice(4 * h, 4 * h + 4))) for h in range(2)]
        scales.append(jnp.concatenate([jnp.broadcast_to(v, (1, 128)) for v in pair], axis=1))
        wide = [jnp.broadcast_to(UNIT / v, (8, 128)) for v in pair]
        factors.append(jnp.where(sub < 4, wide[0], wide[1]))

    def quantize(m):
        factor = factors[m][None]

        def values(p, yh, yl):
            block = codes[p, yh, :, yl, :, m].reshape(zhs * 2, 8, 128)
            return level_value(block.astype(jnp.int32).astype(jnp.float32), factor)

        def step(t, carry):
            y = t // xs
            x = t % xs
            even = values(2 * x, y // 2, y % 2)
            odd = values(2 * x + 1, y // 2, y % 2)
            first_half = (lax.broadcasted_iota(jnp.int32, even.shape, 1)) < 4
            left = jnp.where(first_half, even, pltpu.roll(odd, 4, 1))
            right = jnp.where(first_half, pltpu.roll(even, 4, 1), odd)
            span = pl.ds(pl.multiple_of(t * 64, 64), 64)
            packed[m, span, 0:128] = snap(left.reshape(64, 128))
            packed[m, span, 128:256] = snap(right.reshape(64, 128))
            return carry

        lax.fori_loop(0, xs * yhs * 2, step, 0, unroll=xs * yhs * 2)

    for m in range(2):
        quantize(m)
    gate_act = jnp.zeros((rows, 256), jnp.float32)
    up_act = jnp.zeros((rows, 256), jnp.float32)
    half = packed.shape[1] // 2
    for part, own in ((near, place[0]), (far, 1 - place[0])):
        level = part[...].astype(jnp.int32).astype(jnp.float32)
        lines[...] = level_value(level, TOKEN_UNIT).reshape(lines.shape)
        token_rows = jnp.concatenate(
            [lines[pl.ds(k, rows, 8), :].astype(jnp.bfloat16) for k in range(8)], axis=1
        )
        features = pl.ds(pl.multiple_of(own * half, half), half)
        gate_act += jnp.dot(token_rows, packed[0, features], preferred_element_type=jnp.float32)
        up_act += jnp.dot(token_rows, packed[1, features], preferred_element_type=jnp.float32)
    gate_act = gate_act * scales[0]
    up_act = up_act * scales[1]
    act = gate_act / (1.0 + jnp.exp(-gate_act)) * up_act
    out[0:rows] = encode(act, ACT_BOUND, 7).astype(jnp.int16)
    levels = [block_level(top[2], slice(2 * b, 2 * b + 2)) for b in range(4)]
    line = jnp.concatenate([jnp.broadcast_to(v, (16, 64)) for v in levels], axis=1)
    out[rows : rows + 16] = line.astype(jnp.int32).astype(jnp.int16)


def gate_up(place, codes, near, far):
    sources = near.shape[0]
    width = 2 * 8 * 128
    vmem = pl.BlockSpec(memory_space=pltpu.VMEM)
    return pl.pallas_call(
        gate_kernel,
        out_shape=jax.ShapeDtypeStruct((sources * CAP + 16, 256), jnp.int16),
        in_specs=[pl.BlockSpec(memory_space=pltpu.SMEM), vmem, vmem, vmem],
        out_specs=vmem,
        scratch_shapes=[
            pltpu.VMEM((2, width, 256), jnp.bfloat16),
            pltpu.VMEM((sources * CAP * 8, 128), jnp.float32),
        ],
        compiler_params=pltpu.CompilerParams(vmem_limit_bytes=20 * 2**20),
    )(place, codes, near, far)


def down_kernel(codes, acts, out, packed, spread):
    copies = codes.shape[0]
    xs, yhs, zhs = copies // 2, codes.shape[1], codes.shape[2]
    rows = acts.shape[1] - 16
    sub = lax.broadcasted_iota(jnp.int32, (8, 128), 0)
    marks = acts[:, rows : rows + 16].astype(jnp.int32).astype(jnp.float32)
    line = jnp.max(jnp.maximum(marks[0], marks[1]), axis=0, keepdims=True)
    level = acts[:, 0:rows].astype(jnp.int32).astype(jnp.float32)
    square = level * level
    act = (square * square * square * level * ACT_UNIT).astype(jnp.bfloat16)
    scales = [None] * 4
    factor = jnp.zeros((8, 128), jnp.float32)
    for h in range(2):
        for t in range(2):
            b = 2 * h + t
            scale = scale_of(jnp.max(line[:, b * 64 : (b + 1) * 64], axis=1, keepdims=True))
            scales[2 * t + h] = scale
            factor = jnp.where(sub // 2 == b, jnp.broadcast_to(UNIT / scale, (8, 128)), factor)
    factor = factor[None]
    low_pair = (lax.broadcasted_iota(jnp.int32, (zhs, 8, 128), 1)) % 4 < 2
    low_half = (lax.broadcasted_iota(jnp.int32, (zhs, 8, 128), 1)) < 4

    def values(p, yh, yl, zl):
        block = codes[p, yh, :, yl, zl, 2]
        return level_value(block.astype(jnp.int32).astype(jnp.float32), factor)

    def step(i, carry):
        y = i // xs
        x = i % xs
        yh, yl = y // 2, y % 2
        by_t = []
        for zl in range(2):
            even = values(2 * x, yh, yl, zl)
            odd = values(2 * x + 1, yh, yl, zl)
            by_t.append(
                (
                    jnp.where(low_pair, even, pltpu.roll(odd, 2, 1)),
                    jnp.where(low_pair, pltpu.roll(even, 6, 1), odd),
                )
            )
        span = pl.ds(pl.multiple_of(i * zhs * 8, zhs * 8), zhs * 8)
        for t in range(2):
            near, far = by_t[0][t], by_t[1][t]
            top = jnp.where(low_half, near, pltpu.roll(far, 4, 1))
            bottom = jnp.where(low_half, pltpu.roll(near, 4, 1), far)
            packed[span, 256 * t : 256 * t + 128] = snap(top.reshape(zhs * 8, 128))
            packed[span, 256 * t + 128 : 256 * t + 256] = snap(bottom.reshape(zhs * 8, 128))
        return carry

    lax.fori_loop(0, xs * yhs * 2, step, 0, unroll=8)
    partial_value = jnp.zeros((rows, packed.shape[0]), jnp.float32)
    for b in range(4):
        partial_value += scales[b] * lax.dot_general(
            act[b // 2, :, 128 * (b % 2) : 128 * (b % 2) + 128],
            packed[:, 128 * b : 128 * b + 128],
            (((1,), (1,)), ((), ())),
            preferred_element_type=jnp.float32,
        )
    blocks = out.shape[1] // CAP
    for k in range(blocks):
        spread[pl.ds(k, rows, blocks), :] = partial_value[:, k * 128 : (k + 1) * 128]
    out[...] = spread[...].reshape(out.shape).astype(jnp.bfloat16)


def down(codes, acts):
    sources = (acts.shape[1] - 16) // CAP
    lines = CAP * 8
    vmem = pl.BlockSpec(memory_space=pltpu.VMEM)
    return pl.pallas_call(
        down_kernel,
        out_shape=jax.ShapeDtypeStruct((sources, lines, 128), jnp.bfloat16),
        in_specs=[vmem, vmem],
        out_specs=vmem,
        scratch_shapes=[
            pltpu.VMEM((lines // CAP * 128, 512), jnp.bfloat16),
            pltpu.VMEM((sources * lines, 128), jnp.float32),
        ],
        compiler_params=pltpu.CompilerParams(vmem_limit_bytes=20 * 2**20),
    )(codes, acts)


def combine_kernel(returned, weighted, out, total):
    experts, lines = returned.shape[0], returned.shape[3]
    width = lines // CAP
    rows = weighted.shape[0]
    weights = weighted[...]
    sums = [[jnp.zeros((width, 128), jnp.float32) for _ in range(rows)] for _ in range(2)]
    for e in range(experts):
        for j in range(CAP):
            slot = e * CAP + j
            for zl in range(2):
                value = returned[e, 0, zl, j * width : (j + 1) * width].astype(jnp.float32)
                value = value + returned[e, 1, zl, j * width : (j + 1) * width].astype(jnp.float32)
                for t in range(rows):
                    sums[zl][t] = sums[zl][t] + weights[t : t + 1, slot : slot + 1] * value
    source = lax.broadcasted_iota(jnp.int32, (128, 256), 0)
    target = lax.broadcasted_iota(jnp.int32, (128, 256), 1)
    placed = jnp.zeros((rows * width, 256), jnp.float32)
    for zl in range(2):
        spot = (target == source // 2 * 4 + 2 * zl + source % 2).astype(jnp.float32).astype(jnp.bfloat16)
        halves = jnp.concatenate(sums[zl], axis=0).astype(jnp.bfloat16)
        placed += jnp.dot(halves, spot, preferred_element_type=jnp.float32)
    total[0] = placed[:, 0:128]
    total[1] = placed[:, 128:256]
    for k in range(width):
        for h in range(2):
            out[:, k * 256 + h * 128 : k * 256 + h * 128 + 128] = total[
                h, pl.ds(k, rows, width), :
            ].astype(jnp.bfloat16)


def combine(returned, weighted):
    rows = weighted.shape[0]
    width = returned.shape[3] // CAP
    vmem = pl.BlockSpec(memory_space=pltpu.VMEM)
    return pl.pallas_call(
        combine_kernel,
        out_shape=jax.ShapeDtypeStruct((rows, width * 256), jnp.bfloat16),
        in_specs=[vmem, vmem],
        out_specs=vmem,
        scratch_shapes=[pltpu.VMEM((2, rows * width, 128), jnp.float32)],
        compiler_params=pltpu.CompilerParams(vmem_limit_bytes=16 * 2**20),
    )(returned, weighted)


def body(master, moment_one, moment_two, gradient, states, norm_gain, routes, route_weights):
    owners = lax.axis_size(OWNERS)
    state = [to_tiles(array) for array in (master, moment_one, moment_two, gradient)]
    updated, codes, weighted = prepare(
        *state, states, norm_gain[None, :], routes, route_weights, owners
    )
    received = lax.all_to_all(codes, OWNERS, split_axis=0, concat_axis=0, tiled=True)
    near = received[:, 3:]
    far = lax.ppermute(near, "zl", [(0, 1), (1, 0)])
    gathered = lax.all_gather(received[:, :3], COPIES, axis=0, tiled=False)
    place = lax.axis_index("zl").astype(jnp.int32).reshape(1)
    gathered = gathered.reshape(-1, 4, 4, 2, 2, 3, 8, 128)
    acts = lax.all_gather(gate_up(place, gathered, near, far), "zl", axis=0, tiled=False)
    partial_value = down(gathered, acts)
    returned = lax.all_to_all(partial_value, OWNERS, split_axis=0, concat_axis=0, tiled=True)
    mixture = combine(returned.reshape(E, 2, 2, -1, 128), weighted)
    return (from_tiles(updated), mixture)


def solution(mesh):
    chips = Mesh(mesh.devices.reshape(4, 2, 4, 4, 2, 2), AXES)
    rows = P(None, AXES, None)
    return jax.shard_map(
        body,
        mesh=chips,
        in_specs=(rows, rows, rows, rows, P(AXES, None), P(), P(AXES, None), P(AXES, None)),
        out_specs=(rows, P(AXES, None)),
        check_vma=False,
    )
```

```python
import jax
import jax.numpy as jnp
from jax import lax
from jax.experimental import pallas as pl
from jax.experimental.pallas import tpu as pltpu
from jax.sharding import Mesh, PartitionSpec as P

E = 16
TOP = 8
QBLOCK = 128
STEP = 10
CAP = 3

BETA_ONE = 0.9
BETA_TWO = 0.95
LEARN_RATE = 0.01
ADAM_EPSILON = 1e-08
WEIGHT_DECAY = 0.1
SATURATION = 448.0
SCALE_EPSILON = 1e-06
NORM_EPSILON = 1e-06

BOUND = 0.1875
LEVELS = 32767.0
UNIT = BOUND / LEVELS**5

TOKEN_BOUND = 68.0
TOKEN_UNIT = TOKEN_BOUND / LEVELS**5
ACT_BOUND = 524288.0
ACT_UNIT = ACT_BOUND / LEVELS**7

AXES = ("yh", "yl", "x", "zh", "zl", "c")
OWNERS = ("yh", "zh", "yl", "zl")
COPIES = ("x", "c")


def adam_tile(master, moment_one, moment_two, grad_float):
    correct_one = LEARN_RATE / (1.0 - BETA_ONE**STEP)
    correct_two = 1.0 / (1.0 - BETA_TWO**STEP)
    first = (BETA_ONE * correct_one) * moment_one + ((1.0 - BETA_ONE) * correct_one) * grad_float
    second = (BETA_TWO * correct_two) * moment_two + (
        ((1.0 - BETA_TWO) * correct_two) * grad_float * grad_float
    )
    spread = second * lax.rsqrt(second) + ADAM_EPSILON
    inverse = pl.reciprocal(spread, approx=True)
    inverse = inverse * (2.0 - spread * inverse)
    return (1.0 - LEARN_RATE * WEIGHT_DECAY) * master - first * inverse


def encode(values, bound, power=5):
    magnitude = jnp.maximum(jnp.abs(values) * (1.0 / bound), 1e-35)
    level = jnp.minimum(jnp.exp2(jnp.log2(magnitude) * (1.0 / power)) * LEVELS + 0.5, LEVELS)
    return jnp.where(values < 0, -level, level).astype(jnp.int32)


def dispatch(states, norm_gain, routes, route_weights, weighted, lines, chosen):
    rows, width = states.shape
    blocks = width // 128
    values = states[...].astype(jnp.float32)
    mean_square = jnp.mean(values * values, axis=1, keepdims=True)
    normed = values * lax.rsqrt(mean_square + NORM_EPSILON) * norm_gain[...]
    level = encode(normed, TOKEN_BOUND).astype(jnp.float32)
    for k in range(blocks):
        lines[pl.ds(k, rows, blocks), :] = level[:, k * 128 : (k + 1) * 128]

    lane = lax.broadcasted_iota(jnp.int32, (rows, 128), 1)
    expert = lane // CAP
    ids = routes[...]
    gains = route_weights[...]
    gains = gains / jnp.sum(gains, axis=1, keepdims=True)
    named = jnp.zeros((rows, 128), jnp.float32)
    gain = jnp.zeros((rows, 128), jnp.float32)
    for k in range(TOP):
        hit = ids[:, k : k + 1] == expert
        named = jnp.where(hit, 1.0, named)
        gain = jnp.where(hit, gains[:, k : k + 1], gain)
    slot = (lane - expert * CAP).astype(jnp.float32)
    earlier = jnp.zeros((1, 128), jnp.float32)
    picks = []
    for t in range(rows):
        pick = jnp.where(earlier == slot[t : t + 1], named[t : t + 1], 0.0)
        weighted[t : t + 1, :] = pick * gain[t : t + 1]
        picks.append(pick)
        earlier = earlier + named[t : t + 1]
    tiles = [lines[t * blocks : (t + 1) * blocks] for t in range(rows)]
    for n in range(E * CAP):
        row = picks[0][:, n : n + 1] * tiles[0]
        for t in range(1, rows):
            row = row + picks[t][:, n : n + 1] * tiles[t]
        chosen[n] = row.astype(jnp.int32).astype(jnp.int16).reshape(2, 8, 128)


def owner_kernel(
    master, moment_one, moment_two, gradient, states, norm_gain, routes, route_weights,
    updated, codes, weighted, lines, chosen,
):
    step = pl.program_id(0)

    @pl.when(step == 0)
    def _():
        dispatch(states, norm_gain, routes, route_weights, weighted, lines, chosen)

    pair_rows = lax.broadcasted_iota(jnp.int32, (8, 128), 0) % 4 < 2
    group = 8

    def some(i, carry):
        down = []
        for d in range(group):
            owner = i * group + d
            for m in range(3):
                value = adam_tile(
                    master[m, owner], moment_one[m, owner], moment_two[m, owner],
                    gradient[m, owner].astype(jnp.float32),
                )
                updated[m, owner] = value
                if m < 2:
                    codes[owner, m] = encode(value, BOUND).astype(jnp.int16)
                else:
                    down.append(encode(value, BOUND))
            if d % 2:
                first, second = down[d - 1], down[d]
                low = jnp.where(pair_rows, first, pltpu.roll(second, 2, 0))
                high = jnp.where(pair_rows, pltpu.roll(first, 6, 0), second)
                codes[owner - 1, 2] = low.astype(jnp.int16)
                codes[owner, 2] = high.astype(jnp.int16)
            slot = (step * (codes.shape[0] // 4) + i * (group // 4) + d // 4) * CAP
            for j in range(CAP):
                codes[owner, 3 + j] = chosen[slot + j, d % 2]
        return carry

    lax.fori_loop(0, codes.shape[0] // group, some, 0)


def prepare(master, moment_one, moment_two, gradient, states, norm_gain, routes, route_weights, owners):
    steps = 2
    rows = pl.BlockSpec((3, owners // steps, 8, 128), lambda i: (0, i, 0, 0))
    whole = lambda array: pl.BlockSpec(array.shape, lambda i: (0, 0))
    count, width = states.shape
    small = (states, norm_gain, routes, route_weights)
    return pl.pallas_call(
        owner_kernel,
        grid=(steps,),
        out_shape=(
            jax.ShapeDtypeStruct(master.shape, jnp.float32),
            jax.ShapeDtypeStruct((owners, 3 + CAP, 8, 128), jnp.int16),
            jax.ShapeDtypeStruct((count, 128), jnp.float32),
        ),
        in_specs=[rows] * 4 + [whole(array) for array in small],
        out_specs=(
            rows,
            pl.BlockSpec((owners // steps, 3 + CAP, 8, 128), lambda i: (i, 0, 0, 0)),
            pl.BlockSpec((count, 128), lambda i: (0, 0)),
        ),
        scratch_shapes=[
            pltpu.VMEM((count * width // 128, 128), jnp.float32),
            pltpu.VMEM((E * CAP, 2, 8, 128), jnp.int16),
        ],
        compiler_params=pltpu.CompilerParams(vmem_limit_bytes=60 * 2**20),
    )(master, moment_one, moment_two, gradient, *small)


def to_tiles(array):
    matrices, rows, columns = array.shape
    parts = array.reshape(matrices, rows, columns // 256, 2, 128).transpose(0, 2, 3, 1, 4)
    return parts.reshape(matrices, columns // 256, 2 * rows, 128)


def from_tiles(tiles):
    matrices, owners = tiles.shape[:2]
    parts = tiles.reshape(matrices, owners, 2, 4, 128).transpose(0, 3, 1, 2, 4)
    return parts.reshape(matrices, 4, owners * 256)


def snap(q):
    clipped = jnp.clip(q, -SATURATION, SATURATION)
    return clipped.astype(jnp.float8_e4m3fn).astype(jnp.bfloat16)


def level_value(level, unit):
    square = level * level
    return square * square * level * unit


def block_level(top, rows):
    return jnp.max(jnp.max(top[rows], axis=0, keepdims=True), axis=1, keepdims=True)


def scale_of(level):
    return (level_value(level, UNIT) + SCALE_EPSILON) / SATURATION


def gate_kernel(place, codes, near, far, out, packed, lines):
    copies = codes.shape[0]
    xs, yhs, zhs = copies // 2, codes.shape[1], codes.shape[2]
    rows = near.shape[0] * CAP

    def extremes(step, carry):
        high, low = carry
        p = step // yhs
        yh = step % yhs
        block = codes[p, yh].astype(jnp.int32).reshape(zhs * 4, 3, 8, 128)
        return jnp.maximum(high, jnp.max(block, axis=0)), jnp.minimum(low, jnp.min(block, axis=0))

    zero = jnp.zeros((3, 8, 128), jnp.int32)
    high, low = lax.fori_loop(0, copies * yhs, extremes, (zero, zero), unroll=32)
    top = jnp.maximum(high, -low).astype(jnp.float32)
    sub = lax.broadcasted_iota(jnp.int32, (8, 128), 0)
    scales = []
    factors = []
    for m in range(2):
        pair = [scale_of(block_level(top[m], slice(4 * h, 4 * h + 4))) for h in range(2)]
        scales.append(jnp.concatenate([jnp.broadcast_to(v, (1, 128)) for v in pair], axis=1))
        wide = [jnp.broadcast_to(UNIT / v, (8, 128)) for v in pair]
        factors.append(jnp.where(sub < 4, wide[0], wide[1]))

    def quantize(m):
        factor = factors[m][None]

        def values(p, yh, yl):
            block = codes[p, yh, :, yl, :, m].reshape(zhs * 2, 8, 128)
            return level_value(block.astype(jnp.int32).astype(jnp.float32), factor)

        def step(t, carry):
            y = t // xs
            x = t % xs
            even = values(2 * x, y // 2, y % 2)
            odd = values(2 * x + 1, y // 2, y % 2)
            first_half = (lax.broadcasted_iota(jnp.int32, even.shape, 1)) < 4
            left = jnp.where(first_half, even, pltpu.roll(odd, 4, 1))
            right = jnp.where(first_half, pltpu.roll(even, 4, 1), odd)
            span = pl.ds(pl.multiple_of(t * 64, 64), 64)
            packed[m, span, 0:128] = snap(left.reshape(64, 128))
            packed[m, span, 128:256] = snap(right.reshape(64, 128))
            return carry

        lax.fori_loop(0, xs * yhs * 2, step, 0, unroll=xs * yhs * 2)

    half = packed.shape[1] // 2
    parts = []
    for part, own in ((near, place[0]), (far, 1 - place[0])):
        level = part[...].astype(jnp.int32).astype(jnp.float32)
        lines[...] = level_value(level, TOKEN_UNIT).reshape(lines.shape)
        token_rows = jnp.concatenate(
            [lines[pl.ds(k, rows, 8), :].astype(jnp.bfloat16) for k in range(8)], axis=1
        )
        features = pl.ds(pl.multiple_of(own * half, half), half)
        parts.append((token_rows, features))
    sums = []
    for m in range(2):
        quantize(m)
        act = jnp.zeros((rows, 256), jnp.float32)
        for token_rows, features in parts:
            act += jnp.dot(token_rows, packed[m, features], preferred_element_type=jnp.float32)
        sums.append(act)
    gate_act, up_act = sums
    gate_act = gate_act * scales[0]
    up_act = up_act * scales[1]
    act = gate_act / (1.0 + jnp.exp(-gate_act)) * up_act
    out[0:rows] = encode(act, ACT_BOUND, 7).astype(jnp.int16)
    levels = [block_level(top[2], slice(2 * b, 2 * b + 2)) for b in range(4)]
    line = jnp.concatenate([jnp.broadcast_to(v, (16, 64)) for v in levels], axis=1)
    out[rows : rows + 16] = line.astype(jnp.int32).astype(jnp.int16)


def gate_up(place, codes, near, far):
    sources = near.shape[0]
    width = 2 * 8 * 128
    vmem = pl.BlockSpec(memory_space=pltpu.VMEM)
    return pl.pallas_call(
        gate_kernel,
        out_shape=jax.ShapeDtypeStruct((sources * CAP + 16, 256), jnp.int16),
        in_specs=[pl.BlockSpec(memory_space=pltpu.SMEM), vmem, vmem, vmem],
        out_specs=vmem,
        scratch_shapes=[
            pltpu.VMEM((2, width, 256), jnp.bfloat16),
            pltpu.VMEM((sources * CAP * 8, 128), jnp.float32),
        ],
        compiler_params=pltpu.CompilerParams(vmem_limit_bytes=20 * 2**20),
    )(place, codes, near, far)


def down_kernel(codes, acts, out, packed, spread):
    copies = codes.shape[0]
    xs, yhs, zhs = copies // 2, codes.shape[1], codes.shape[2]
    rows = acts.shape[1] - 16
    sub = lax.broadcasted_iota(jnp.int32, (8, 128), 0)
    marks = acts[:, rows : rows + 16].astype(jnp.int32).astype(jnp.float32)
    line = jnp.max(jnp.maximum(marks[0], marks[1]), axis=0, keepdims=True)
    level = acts[:, 0:rows].astype(jnp.int32).astype(jnp.float32)
    square = level * level
    act = (square * square * square * level * ACT_UNIT).astype(jnp.bfloat16)
    scales = [None] * 4
    factor = jnp.zeros((8, 128), jnp.float32)
    for h in range(2):
        for t in range(2):
            b = 2 * h + t
            scale = scale_of(jnp.max(line[:, b * 64 : (b + 1) * 64], axis=1, keepdims=True))
            scales[2 * t + h] = scale
            factor = jnp.where(sub // 2 == b, jnp.broadcast_to(UNIT / scale, (8, 128)), factor)
    factor = factor[None]
    low_pair = (lax.broadcasted_iota(jnp.int32, (zhs, 8, 128), 1)) % 4 < 2
    low_half = (lax.broadcasted_iota(jnp.int32, (zhs, 8, 128), 1)) < 4

    def values(p, yh, yl, zl):
        block = codes[p, yh, :, yl, zl, 2]
        return level_value(block.astype(jnp.int32).astype(jnp.float32), factor)

    def step(i, carry):
        y = i // xs
        x = i % xs
        yh, yl = y // 2, y % 2
        by_t = []
        for zl in range(2):
            even = values(2 * x, yh, yl, zl)
            odd = values(2 * x + 1, yh, yl, zl)
            by_t.append(
                (
                    jnp.where(low_pair, even, pltpu.roll(odd, 2, 1)),
                    jnp.where(low_pair, pltpu.roll(even, 6, 1), odd),
                )
            )
        span = pl.ds(pl.multiple_of(i * zhs * 8, zhs * 8), zhs * 8)
        for t in range(2):
            near, far = by_t[0][t], by_t[1][t]
            top = jnp.where(low_half, near, pltpu.roll(far, 4, 1))
            bottom = jnp.where(low_half, pltpu.roll(near, 4, 1), far)
            packed[span, 256 * t : 256 * t + 128] = snap(top.reshape(zhs * 8, 128))
            packed[span, 256 * t + 128 : 256 * t + 256] = snap(bottom.reshape(zhs * 8, 128))
        return carry

    lax.fori_loop(0, xs * yhs * 2, step, 0, unroll=32)
    partial_value = jnp.zeros((rows, packed.shape[0]), jnp.float32)
    for b in range(4):
        partial_value += scales[b] * lax.dot_general(
            act[b // 2, :, 128 * (b % 2) : 128 * (b % 2) + 128],
            packed[:, 128 * b : 128 * b + 128],
            (((1,), (1,)), ((), ())),
            preferred_element_type=jnp.float32,
        )
    blocks = out.shape[1] // CAP
    for k in range(blocks):
        spread[pl.ds(k, rows, blocks), :] = partial_value[:, k * 128 : (k + 1) * 128]
    out[...] = spread[...].reshape(out.shape).astype(jnp.bfloat16)


def down(codes, acts):
    sources = (acts.shape[1] - 16) // CAP
    lines = CAP * 8
    vmem = pl.BlockSpec(memory_space=pltpu.VMEM)
    return pl.pallas_call(
        down_kernel,
        out_shape=jax.ShapeDtypeStruct((sources, lines, 128), jnp.bfloat16),
        in_specs=[vmem, vmem],
        out_specs=vmem,
        scratch_shapes=[
            pltpu.VMEM((lines // CAP * 128, 512), jnp.bfloat16),
            pltpu.VMEM((sources * lines, 128), jnp.float32),
        ],
        compiler_params=pltpu.CompilerParams(vmem_limit_bytes=20 * 2**20),
    )(codes, acts)


def combine_kernel(returned, weighted, out, total):
    experts, lines = returned.shape[0], returned.shape[3]
    width = lines // CAP
    rows = weighted.shape[0]
    weights = weighted[...]
    sums = [[jnp.zeros((width, 128), jnp.float32) for _ in range(rows)] for _ in range(2)]
    for e in range(experts):
        for j in range(CAP):
            slot = e * CAP + j
            for zl in range(2):
                value = returned[e, 0, zl, j * width : (j + 1) * width].astype(jnp.float32)
                value = value + returned[e, 1, zl, j * width : (j + 1) * width].astype(jnp.float32)
                for t in range(rows):
                    sums[zl][t] = sums[zl][t] + weights[t : t + 1, slot : slot + 1] * value
    source = lax.broadcasted_iota(jnp.int32, (128, 256), 0)
    target = lax.broadcasted_iota(jnp.int32, (128, 256), 1)
    placed = jnp.zeros((rows * width, 256), jnp.float32)
    for zl in range(2):
        spot = (target == source // 2 * 4 + 2 * zl + source % 2).astype(jnp.float32).astype(jnp.bfloat16)
        halves = jnp.concatenate(sums[zl], axis=0).astype(jnp.bfloat16)
        placed += jnp.dot(halves, spot, preferred_element_type=jnp.float32)
    total[0] = placed[:, 0:128]
    total[1] = placed[:, 128:256]
    for k in range(width):
        for h in range(2):
            out[:, k * 256 + h * 128 : k * 256 + h * 128 + 128] = total[
                h, pl.ds(k, rows, width), :
            ].astype(jnp.bfloat16)


def combine(returned, weighted):
    rows = weighted.shape[0]
    width = returned.shape[3] // CAP
    vmem = pl.BlockSpec(memory_space=pltpu.VMEM)
    return pl.pallas_call(
        combine_kernel,
        out_shape=jax.ShapeDtypeStruct((rows, width * 256), jnp.bfloat16),
        in_specs=[vmem, vmem],
        out_specs=vmem,
        scratch_shapes=[pltpu.VMEM((2, rows * width, 128), jnp.float32)],
        compiler_params=pltpu.CompilerParams(vmem_limit_bytes=16 * 2**20),
    )(returned, weighted)


def body(master, moment_one, moment_two, gradient, states, norm_gain, routes, route_weights):
    owners = lax.axis_size(OWNERS)
    state = [to_tiles(array) for array in (master, moment_one, moment_two, gradient)]
    updated, codes, weighted = prepare(
        *state, states, norm_gain[None, :], routes, route_weights, owners
    )
    received = lax.all_to_all(codes, OWNERS, split_axis=0, concat_axis=0, tiled=True)
    near = received[:, 3:]
    far = lax.ppermute(near, "zl", [(0, 1), (1, 0)])
    gathered = lax.all_gather(received[:, :3], COPIES, axis=0, tiled=False)
    place = lax.axis_index("zl").astype(jnp.int32).reshape(1)
    gathered = gathered.reshape(-1, 4, 4, 2, 2, 3, 8, 128)
    acts = lax.all_gather(gate_up(place, gathered, near, far), "zl", axis=0, tiled=False)
    partial_value = down(gathered, acts)
    returned = lax.all_to_all(partial_value, OWNERS, split_axis=0, concat_axis=0, tiled=True)
    mixture = combine(returned.reshape(E, 2, 2, -1, 128), weighted)
    return (from_tiles(updated), mixture)


def solution(mesh):
    chips = Mesh(mesh.devices.reshape(4, 2, 4, 4, 2, 2), AXES)
    rows = P(None, AXES, None)
    return jax.shard_map(
        body,
        mesh=chips,
        in_specs=(rows, rows, rows, rows, P(AXES, None), P(), P(AXES, None), P(AXES, None)),
        out_specs=(rows, P(AXES, None)),
        check_vma=False,
    )
```

```python
import jax
import jax.numpy as jnp
from jax import lax
from jax.experimental import pallas as pl
from jax.experimental.pallas import tpu as pltpu
from jax.sharding import Mesh, PartitionSpec as P

E = 16
TOP = 8
QBLOCK = 128
STEP = 10
CAP = 3

BETA_ONE = 0.9
BETA_TWO = 0.95
LEARN_RATE = 0.01
ADAM_EPSILON = 1e-08
WEIGHT_DECAY = 0.1
SATURATION = 448.0
SCALE_EPSILON = 1e-06
NORM_EPSILON = 1e-06

BOUND = 0.1875
LEVELS = 32767.0
UNIT = BOUND / LEVELS**5

TOKEN_BOUND = 68.0
TOKEN_UNIT = TOKEN_BOUND / LEVELS**5
ACT_BOUND = 524288.0
ACT_UNIT = ACT_BOUND / LEVELS**7

AXES = ("yh", "yl", "x", "zh", "zl", "c")
OWNERS = ("yl", "yh", "zl", "zh")
COPIES = ("x", "c")


def adam_tile(master, moment_one, moment_two, grad_float):
    correct_one = LEARN_RATE / (1.0 - BETA_ONE**STEP)
    correct_two = 1.0 / (1.0 - BETA_TWO**STEP)
    first = (BETA_ONE * correct_one) * moment_one + ((1.0 - BETA_ONE) * correct_one) * grad_float
    second = (BETA_TWO * correct_two) * moment_two + (
        ((1.0 - BETA_TWO) * correct_two) * grad_float * grad_float
    )
    spread = second * lax.rsqrt(second) + ADAM_EPSILON
    inverse = pl.reciprocal(spread, approx=True)
    inverse = inverse * (2.0 - spread * inverse)
    return (1.0 - LEARN_RATE * WEIGHT_DECAY) * master - first * inverse


def encode(values, bound, power=5):
    magnitude = jnp.maximum(jnp.abs(values) * (1.0 / bound), 1e-35)
    level = jnp.minimum(jnp.exp2(jnp.log2(magnitude) * (1.0 / power)) * LEVELS + 0.5, LEVELS)
    return jnp.where(values < 0, -level, level).astype(jnp.int32)


def dispatch(states, norm_gain, routes, route_weights, weighted, lines, chosen):
    rows, width = states.shape
    blocks = width // 128
    values = states[...].astype(jnp.float32)
    mean_square = jnp.mean(values * values, axis=1, keepdims=True)
    normed = values * lax.rsqrt(mean_square + NORM_EPSILON) * norm_gain[...]
    level = encode(normed, TOKEN_BOUND).astype(jnp.float32)
    for k in range(blocks):
        lines[pl.ds(k, rows, blocks), :] = level[:, k * 128 : (k + 1) * 128]

    lane = lax.broadcasted_iota(jnp.int32, (rows, 128), 1)
    expert = lane // CAP
    ids = routes[...]
    gains = route_weights[...]
    gains = gains / jnp.sum(gains, axis=1, keepdims=True)
    named = jnp.zeros((rows, 128), jnp.float32)
    gain = jnp.zeros((rows, 128), jnp.float32)
    for k in range(TOP):
        hit = ids[:, k : k + 1] == expert
        named = jnp.where(hit, 1.0, named)
        gain = jnp.where(hit, gains[:, k : k + 1], gain)
    slot = (lane - expert * CAP).astype(jnp.float32)
    earlier = jnp.zeros((1, 128), jnp.float32)
    picks = []
    for t in range(rows):
        pick = jnp.where(earlier == slot[t : t + 1], named[t : t + 1], 0.0)
        weighted[t : t + 1, :] = pick * gain[t : t + 1]
        picks.append(pick)
        earlier = earlier + named[t : t + 1]
    tiles = [lines[t * blocks : (t + 1) * blocks] for t in range(rows)]
    for n in range(E * CAP):
        row = picks[0][:, n : n + 1] * tiles[0]
        for t in range(1, rows):
            row = row + picks[t][:, n : n + 1] * tiles[t]
        chosen[n] = row.astype(jnp.int32).astype(jnp.int16).reshape(2, 8, 128)


def owner_kernel(
    master, moment_one, moment_two, gradient, states, norm_gain, routes, route_weights,
    updated, codes, weighted, lines, chosen,
):
    step = pl.program_id(0)

    @pl.when(step == 0)
    def _():
        dispatch(states, norm_gain, routes, route_weights, weighted, lines, chosen)

    pair_rows = lax.broadcasted_iota(jnp.int32, (8, 128), 0) % 4 < 2
    group = 8

    def some(i, carry):
        down = []
        for d in range(group):
            owner = i * group + d
            place = (d % 4 // 2, i // 2, d % 2, i % 2 * 2 + d // 4)
            for m in range(3):
                value = adam_tile(
                    master[m, owner], moment_one[m, owner], moment_two[m, owner],
                    gradient[m, owner].astype(jnp.float32),
                )
                updated[m, owner] = value
                if m < 2:
                    codes[(*place, m)] = encode(value, BOUND).astype(jnp.int16)
                else:
                    down.append(encode(value, BOUND))
            if d % 2:
                first, second = down[d - 1], down[d]
                low = jnp.where(pair_rows, first, pltpu.roll(second, 2, 0))
                high = jnp.where(pair_rows, pltpu.roll(first, 6, 0), second)
                codes[(*place[:2], 0, place[3], 2)] = low.astype(jnp.int16)
                codes[(*place, 2)] = high.astype(jnp.int16)
            slot = (step * (master.shape[1] // 4) + i * (group // 4) + d // 4) * CAP
            for j in range(CAP):
                codes[(*place, 3 + j)] = chosen[slot + j, d % 2]
        return carry

    lax.fori_loop(0, master.shape[1] // group, some, 0)


def prepare(master, moment_one, moment_two, gradient, states, norm_gain, routes, route_weights, owners):
    steps = 2
    rows = pl.BlockSpec((3, owners // steps, 8, 128), lambda i: (0, i, 0, 0))
    whole = lambda array: pl.BlockSpec(array.shape, lambda i: (0, 0))
    count, width = states.shape
    small = (states, norm_gain, routes, route_weights)
    return pl.pallas_call(
        owner_kernel,
        grid=(steps,),
        out_shape=(
            jax.ShapeDtypeStruct(master.shape, jnp.float32),
            jax.ShapeDtypeStruct((2, 4, 2, 4, 3 + CAP, 8, 128), jnp.int16),
            jax.ShapeDtypeStruct((count, 128), jnp.float32),
        ),
        in_specs=[rows] * 4 + [whole(array) for array in small],
        out_specs=(
            rows,
            pl.BlockSpec((2, 4 // steps, 2, 4, 3 + CAP, 8, 128), lambda i: (0, i, 0, 0, 0, 0, 0)),
            pl.BlockSpec((count, 128), lambda i: (0, 0)),
        ),
        scratch_shapes=[
            pltpu.VMEM((count * width // 128, 128), jnp.float32),
            pltpu.VMEM((E * CAP, 2, 8, 128), jnp.int16),
        ],
        compiler_params=pltpu.CompilerParams(vmem_limit_bytes=60 * 2**20),
    )(master, moment_one, moment_two, gradient, *small)


def to_tiles(array):
    matrices, rows, columns = array.shape
    parts = array.reshape(matrices, rows, columns // 256, 2, 128).transpose(0, 2, 3, 1, 4)
    return parts.reshape(matrices, columns // 256, 2 * rows, 128)


def from_tiles(tiles):
    matrices, owners = tiles.shape[:2]
    parts = tiles.reshape(matrices, owners, 2, 4, 128).transpose(0, 3, 1, 2, 4)
    return parts.reshape(matrices, 4, owners * 256)


def snap(q):
    clipped = jnp.clip(q, -SATURATION, SATURATION)
    return clipped.astype(jnp.float8_e4m3fn).astype(jnp.bfloat16)


def level_value(level, unit):
    square = level * level
    return square * square * level * unit


def block_level(top, rows):
    return jnp.max(jnp.max(top[rows], axis=0, keepdims=True), axis=1, keepdims=True)


def scale_of(level):
    return (level_value(level, UNIT) + SCALE_EPSILON) / SATURATION


def gate_kernel(place, codes, near, far, out, packed, lines):
    copies = codes.shape[0]
    xs, yhs, zhs = copies // 2, codes.shape[2], codes.shape[4]
    rows = near.shape[0] * CAP

    def extremes(step, carry):
        high, low = carry
        p = step // yhs
        yh = step % yhs
        block = codes[p, :, yh].astype(jnp.int32).reshape(zhs * 4, 3, 8, 128)
        return jnp.maximum(high, jnp.max(block, axis=0)), jnp.minimum(low, jnp.min(block, axis=0))

    zero = jnp.zeros((3, 8, 128), jnp.int32)
    high, low = lax.fori_loop(0, copies * yhs, extremes, (zero, zero), unroll=32)
    top = jnp.maximum(high, -low).astype(jnp.float32)
    sub = lax.broadcasted_iota(jnp.int32, (8, 128), 0)
    scales = []
    factors = []
    for m in range(2):
        pair = [scale_of(block_level(top[m], slice(4 * h, 4 * h + 4))) for h in range(2)]
        scales.append(jnp.concatenate([jnp.broadcast_to(v, (1, 128)) for v in pair], axis=1))
        wide = [jnp.broadcast_to(UNIT / v, (8, 128)) for v in pair]
        factors.append(jnp.where(sub < 4, wide[0], wide[1]))

    def quantize(m):
        factor = factors[m][None]

        def values(p, yh, yl):
            halves = [codes[p, yl, yh, zl, :, m] for zl in range(2)]
            block = jnp.stack(halves, axis=1).reshape(zhs * 2, 8, 128)
            return level_value(block.astype(jnp.int32).astype(jnp.float32), factor)

        def step(t, carry):
            y = t // xs
            x = t % xs
            even = values(2 * x, y // 2, y % 2)
            odd = values(2 * x + 1, y // 2, y % 2)
            first_half = (lax.broadcasted_iota(jnp.int32, even.shape, 1)) < 4
            left = jnp.where(first_half, even, pltpu.roll(odd, 4, 1))
            right = jnp.where(first_half, pltpu.roll(even, 4, 1), odd)
            span = pl.ds(pl.multiple_of(t * 64, 64), 64)
            packed[m, span, 0:128] = snap(left.reshape(64, 128))
            packed[m, span, 128:256] = snap(right.reshape(64, 128))
            return carry

        lax.fori_loop(0, xs * yhs * 2, step, 0, unroll=xs * yhs * 2)

    half = packed.shape[1] // 2
    parts = []
    for part, own in ((near, place[0]), (far, 1 - place[0])):
        level = part[...].astype(jnp.int32).astype(jnp.float32)
        lines[...] = level_value(level, TOKEN_UNIT).reshape(lines.shape)
        token_rows = jnp.concatenate(
            [lines[pl.ds(k, rows, 8), :].astype(jnp.bfloat16) for k in range(8)], axis=1
        )
        features = pl.ds(pl.multiple_of(own * half, half), half)
        parts.append((token_rows, features))
    sums = []
    for m in range(2):
        quantize(m)
        act = jnp.zeros((rows, 256), jnp.float32)
        for token_rows, features in parts:
            act += jnp.dot(token_rows, packed[m, features], preferred_element_type=jnp.float32)
        sums.append(act)
    gate_act, up_act = sums
    gate_act = gate_act * scales[0]
    up_act = up_act * scales[1]
    act = gate_act / (1.0 + jnp.exp(-gate_act)) * up_act
    out[0:rows] = encode(act, ACT_BOUND, 7).astype(jnp.int16)
    levels = [block_level(top[2], slice(2 * b, 2 * b + 2)) for b in range(4)]
    line = jnp.concatenate([jnp.broadcast_to(v, (16, 64)) for v in levels], axis=1)
    out[rows : rows + 16] = line.astype(jnp.int32).astype(jnp.int16)


def gate_up(place, codes, near, far):
    sources = near.shape[0]
    width = 2 * 8 * 128
    vmem = pl.BlockSpec(memory_space=pltpu.VMEM)
    return pl.pallas_call(
        gate_kernel,
        out_shape=jax.ShapeDtypeStruct((sources * CAP + 16, 256), jnp.int16),
        in_specs=[pl.BlockSpec(memory_space=pltpu.SMEM), vmem, vmem, vmem],
        out_specs=vmem,
        scratch_shapes=[
            pltpu.VMEM((2, width, 256), jnp.bfloat16),
            pltpu.VMEM((sources * CAP * 8, 128), jnp.float32),
        ],
        compiler_params=pltpu.CompilerParams(vmem_limit_bytes=20 * 2**20),
    )(place, codes, near, far)


def down_kernel(codes, acts, out, packed, spread):
    copies = codes.shape[0]
    xs, yhs, zhs = copies // 2, codes.shape[2], codes.shape[4]
    rows = acts.shape[1] - 16
    sub = lax.broadcasted_iota(jnp.int32, (8, 128), 0)
    marks = acts[:, rows : rows + 16].astype(jnp.int32).astype(jnp.float32)
    line = jnp.max(jnp.maximum(marks[0], marks[1]), axis=0, keepdims=True)
    level = acts[:, 0:rows].astype(jnp.int32).astype(jnp.float32)
    square = level * level
    act = (square * square * square * level * ACT_UNIT).astype(jnp.bfloat16)
    scales = [None] * 4
    factor = jnp.zeros((8, 128), jnp.float32)
    for h in range(2):
        for t in range(2):
            b = 2 * h + t
            scale = scale_of(jnp.max(line[:, b * 64 : (b + 1) * 64], axis=1, keepdims=True))
            scales[2 * t + h] = scale
            factor = jnp.where(sub // 2 == b, jnp.broadcast_to(UNIT / scale, (8, 128)), factor)
    factor = factor[None]
    low_pair = (lax.broadcasted_iota(jnp.int32, (zhs, 8, 128), 1)) % 4 < 2
    low_half = (lax.broadcasted_iota(jnp.int32, (zhs, 8, 128), 1)) < 4

    def values(p, yh, yl, zl):
        block = codes[p, yl, yh, zl, :, 2]
        return level_value(block.astype(jnp.int32).astype(jnp.float32), factor)

    def step(i, carry):
        y = i // xs
        x = i % xs
        yh, yl = y // 2, y % 2
        by_t = []
        for zl in range(2):
            even = values(2 * x, yh, yl, zl)
            odd = values(2 * x + 1, yh, yl, zl)
            by_t.append(
                (
                    jnp.where(low_pair, even, pltpu.roll(odd, 2, 1)),
                    jnp.where(low_pair, pltpu.roll(even, 6, 1), odd),
                )
            )
        span = pl.ds(pl.multiple_of(i * zhs * 8, zhs * 8), zhs * 8)
        for t in range(2):
            near, far = by_t[0][t], by_t[1][t]
            top = jnp.where(low_half, near, pltpu.roll(far, 4, 1))
            bottom = jnp.where(low_half, pltpu.roll(near, 4, 1), far)
            packed[span, 256 * t : 256 * t + 128] = snap(top.reshape(zhs * 8, 128))
            packed[span, 256 * t + 128 : 256 * t + 256] = snap(bottom.reshape(zhs * 8, 128))
        return carry

    lax.fori_loop(0, xs * yhs * 2, step, 0, unroll=32)
    partial_value = jnp.zeros((rows, packed.shape[0]), jnp.float32)
    for b in range(4):
        partial_value += scales[b] * lax.dot_general(
            act[b // 2, :, 128 * (b % 2) : 128 * (b % 2) + 128],
            packed[:, 128 * b : 128 * b + 128],
            (((1,), (1,)), ((), ())),
            preferred_element_type=jnp.float32,
        )
    blocks = out.shape[1] // CAP
    for k in range(blocks):
        spread[pl.ds(k, rows, blocks), :] = partial_value[:, k * 128 : (k + 1) * 128]
    out[...] = spread[...].reshape(out.shape).astype(jnp.bfloat16)


def down(codes, acts):
    sources = (acts.shape[1] - 16) // CAP
    lines = CAP * 8
    vmem = pl.BlockSpec(memory_space=pltpu.VMEM)
    return pl.pallas_call(
        down_kernel,
        out_shape=jax.ShapeDtypeStruct((sources, lines, 128), jnp.bfloat16),
        in_specs=[vmem, vmem],
        out_specs=vmem,
        scratch_shapes=[
            pltpu.VMEM((lines // CAP * 128, 512), jnp.bfloat16),
            pltpu.VMEM((sources * lines, 128), jnp.float32),
        ],
        compiler_params=pltpu.CompilerParams(vmem_limit_bytes=20 * 2**20),
    )(codes, acts)


def combine_kernel(returned, weighted, out, total):
    experts, lines = E, returned.shape[4]
    width = lines // CAP
    rows = weighted.shape[0]
    weights = weighted[...]
    sums = [[jnp.zeros((width, 128), jnp.float32) for _ in range(rows)] for _ in range(2)]
    for e in range(experts):
        for j in range(CAP):
            slot = e * CAP + j
            for zl in range(2):
                value = returned[0, e // 4, zl, e % 4, j * width : (j + 1) * width].astype(jnp.float32)
                value = value + returned[1, e // 4, zl, e % 4, j * width : (j + 1) * width].astype(jnp.float32)
                for t in range(rows):
                    sums[zl][t] = sums[zl][t] + weights[t : t + 1, slot : slot + 1] * value
    source = lax.broadcasted_iota(jnp.int32, (128, 256), 0)
    target = lax.broadcasted_iota(jnp.int32, (128, 256), 1)
    placed = jnp.zeros((rows * width, 256), jnp.float32)
    for zl in range(2):
        spot = (target == source // 2 * 4 + 2 * zl + source % 2).astype(jnp.float32).astype(jnp.bfloat16)
        halves = jnp.concatenate(sums[zl], axis=0).astype(jnp.bfloat16)
        placed += jnp.dot(halves, spot, preferred_element_type=jnp.float32)
    total[0] = placed[:, 0:128]
    total[1] = placed[:, 128:256]
    for k in range(width):
        for h in range(2):
            out[:, k * 256 + h * 128 : k * 256 + h * 128 + 128] = total[
                h, pl.ds(k, rows, width), :
            ].astype(jnp.bfloat16)


def combine(returned, weighted):
    rows = weighted.shape[0]
    width = returned.shape[4] // CAP
    vmem = pl.BlockSpec(memory_space=pltpu.VMEM)
    return pl.pallas_call(
        combine_kernel,
        out_shape=jax.ShapeDtypeStruct((rows, width * 256), jnp.bfloat16),
        in_specs=[vmem, vmem],
        out_specs=vmem,
        scratch_shapes=[pltpu.VMEM((2, rows * width, 128), jnp.float32)],
        compiler_params=pltpu.CompilerParams(vmem_limit_bytes=16 * 2**20),
    )(returned, weighted)


def body(master, moment_one, moment_two, gradient, states, norm_gain, routes, route_weights):
    owners = lax.axis_size(OWNERS)
    state = [to_tiles(array) for array in (master, moment_one, moment_two, gradient)]
    updated, codes, weighted = prepare(
        *state, states, norm_gain[None, :], routes, route_weights, owners
    )
    codes = codes.reshape(owners, 3 + CAP, 8, 128)
    received = lax.all_to_all(codes, OWNERS, split_axis=0, concat_axis=0, tiled=True)
    near = received[:, 3:]
    far = lax.ppermute(near, "zl", [(0, 1), (1, 0)])
    gathered = lax.all_gather(received[:, :3], COPIES, axis=0, tiled=False)
    place = lax.axis_index("zl").astype(jnp.int32).reshape(1)
    gathered = gathered.reshape(-1, 2, 4, 2, 4, 3, 8, 128)
    acts = lax.all_gather(gate_up(place, gathered, near, far), "zl", axis=0, tiled=False)
    partial_value = down(gathered, acts)
    returned = lax.all_to_all(partial_value, OWNERS, split_axis=0, concat_axis=0, tiled=True)
    mixture = combine(returned.reshape(2, 4, 2, 4, -1, 128), weighted)
    return (from_tiles(updated), mixture)


def solution(mesh):
    chips = Mesh(mesh.devices.reshape(4, 2, 4, 4, 2, 2), AXES)
    rows = P(None, AXES, None)
    return jax.shard_map(
        body,
        mesh=chips,
        in_specs=(rows, rows, rows, rows, P(AXES, None), P(), P(AXES, None), P(AXES, None)),
        out_specs=(rows, P(AXES, None)),
        check_vma=False,
    )
```
